256 devices in a mesh: site: 16 (over y_hi, z), bond: 16 (over x, y_lo, core).
Axes of the slice: x: 4, y: 4 (y_hi: 2, y_lo: 2; y = y_hi * 2 + y_lo), z: 8, core: 2. Of those that a mesh axis runs over, the one named last changes fastest.
Arguments:
- mps: bfloat16 [16, 512, 8, 512], P('site', 'bond'), may hold values from -18 to 18
- projection: bfloat16 [16, 4096, 512], P('site'), may hold values from -1.1 to 1.1
- gates: float32 [16, 64, 64], replicated, may hold values from -1.2 to 1.2
Outputs:
- new_mps: bfloat16 [16, 512, 8, 512], P('site', 'bond')
- pair_log_norm: float32 [16], P('site')
The draws below stay inside these ranges and needn't reach their ends.
All inputs are finite; a program needn't handle non-finite values.
Results may differ from the reference program's by a relative error of at most 0.025.
Values may be sent and summed in bfloat16 or wider, within the bound.
A program may use at most 64 MiB of HBM per device.

```python
import math
import jax
import jax.numpy as jnp
from jax import lax

PHYS = 8
CHI = 512
SITES = 16
N_BOND = 16


def draw_mps(key, part):
    key = jax.random.fold_in(key, 11)
    value_key, row_key = jax.random.split(key)
    shape = (SITES, CHI, PHYS, CHI)
    position = jnp.arange(CHI, dtype=jnp.float32) / (CHI - 1)
    trend = jnp.exp(0.5 * math.log(3.0) * position).reshape(1, CHI, 1, 1)
    left_index = jnp.arange(CHI).reshape(1, CHI, 1, 1)
    right_index = jnp.arange(CHI).reshape(1, 1, 1, CHI)
    state_index = jnp.arange(PHYS).reshape(1, 1, PHYS, 1)
    dominant = jnp.where((left_index == right_index) & (state_index == 0), 1.0, 0.0).astype(jnp.float32)
    values = 0.01 * jax.random.truncated_normal(value_key, -4.0, 4.0, shape, jnp.float32)
    spread = jnp.exp(math.log(3.0) * jax.random.uniform(row_key, (SITES, CHI, 1, 1), jnp.float32))
    return ((dominant + values) * trend * spread).astype(jnp.bfloat16)


def draw_projection(key, part):
    key = jax.random.fold_in(key, 23)
    shape = (SITES, PHYS * CHI, CHI)
    row_index = jnp.arange(PHYS * CHI).reshape(1, PHYS * CHI, 1)
    column_index = jnp.arange(CHI).reshape(1, 1, CHI)
    dominant = jnp.where(row_index == column_index, 1.0, 0.0).astype(jnp.float32)
    values = 0.01 * jax.random.truncated_normal(key, -4.0, 4.0, shape, jnp.float32)
    return (dominant + values).astype(jnp.bfloat16)


def draw_gates(key, part):
    key = jax.random.fold_in(key, 37)
    shape = (SITES, PHYS * PHYS, PHYS * PHYS)
    dominant = jnp.eye(PHYS * PHYS, dtype=jnp.float32).reshape(1, PHYS * PHYS, PHYS * PHYS)
    values = 0.04 * jax.random.truncated_normal(key, -4.0, 4.0, shape, jnp.float32)
    return (dominant + values).astype(jnp.float32)


def setup_inputs(seed: int = 0) -> dict:
    key_list = jax.random.split(jax.random.key(seed), 4)
    mps = draw_mps(jax.random.fold_in(key_list[3], 71), 0)
    projection = draw_projection(jax.random.fold_in(key_list[3], 71), 0)
    gates = draw_gates(jax.random.fold_in(key_list[3], 71), 0)
    return {"mps": mps, "projection": projection, "gates": gates}


epsilon = 1e-06

def pair_update(first, second, sketch_matrix, gate_matrix):
    rows_total = CHI * PHYS
    left_rows = first.reshape(rows_total, CHI)
    raw_theta = jnp.dot(left_rows.astype(jnp.float32), second.reshape(CHI, PHYS * CHI).astype(jnp.float32), preferred_element_type=jnp.float32)
    mixed = raw_theta.reshape(CHI, PHYS * PHYS, CHI)
    gated = jnp.einsum('gh,lhr->lgr', gate_matrix.astype(jnp.float32), mixed, precision=lax.Precision.HIGHEST)
    gated = gated.reshape(rows_total, PHYS * CHI)
    theta_bf = gated.astype(jnp.bfloat16)
    mean_square = jnp.sum(gated * gated) / (CHI * PHYS * PHYS * CHI)
    sketch = jnp.dot(theta_bf.astype(jnp.float32), sketch_matrix.astype(jnp.float32), preferred_element_type=jnp.float32)
    gram_matrix = jnp.dot(sketch.T, sketch, precision=lax.Precision.HIGHEST)
    chol_lower = jnp.linalg.cholesky(gram_matrix)
    ortho = jax.scipy.linalg.solve_triangular(chol_lower, sketch.T, lower=True).T
    gauge_root = math.sqrt(PHYS * CHI)
    left_new = (gauge_root * ortho).astype(jnp.bfloat16)
    norm_scale = lax.rsqrt(mean_square + epsilon)
    block_rows = CHI // N_BOND * PHYS
    summed = jnp.zeros((CHI, PHYS * CHI), jnp.float32)
    for group_id in range(N_BOND):
        part_left = left_new[group_id * block_rows:(group_id + 1) * block_rows]
        part_theta = theta_bf[group_id * block_rows:(group_id + 1) * block_rows]
        partial_term = jnp.dot(part_left.T.astype(jnp.float32), part_theta.astype(jnp.float32), preferred_element_type=jnp.float32) * (norm_scale / gauge_root)
        rounded = lax.optimization_barrier(partial_term.astype(jnp.bfloat16))
        summed = summed + rounded.astype(jnp.float32)
    right_new = summed.astype(jnp.bfloat16).reshape(CHI, PHYS, CHI)
    log_norm = 0.5 * jnp.log(mean_square + epsilon)
    return (left_new.reshape(CHI, PHYS, CHI), right_new, log_norm)

def reference(mps, projection, gates):
    tensors = [mps[site_id] for site_id in range(SITES)]
    log_norms = [jnp.zeros((), jnp.float32) for site_id in range(SITES)]
    for parity in range(2):
        for first_site in range(parity, SITES, 2):
            second_site = (first_site + 1) % SITES
            new_first, new_second, log_norm = pair_update(tensors[first_site], tensors[second_site], projection[first_site], gates[first_site])
            tensors[first_site] = new_first
            tensors[second_site] = new_second
            log_norms[first_site] = log_norm
    return (jnp.stack(tensors), jnp.stack(log_norms))
```

```python
import functools
import math

import jax
import jax.numpy as jnp
from jax import lax
from jax.experimental import pallas as pl
from jax.experimental.pallas import tpu as pltpu
from jax.sharding import PartitionSpec as P

PHYS = 8
CHI = 512
epsilon = 1e-06
MESH = pl.DeviceIdType.MESH
HI = lax.Precision.HIGHEST
F32 = jnp.float32
BF16 = jnp.bfloat16
VMEM = pl.BlockSpec(memory_space=pltpu.VMEM)
ANY = pl.BlockSpec(memory_space=pl.ANY)
VLIM = 56 << 20


def params(cid=None):
    if cid is None:
        return pltpu.CompilerParams(vmem_limit_bytes=VLIM)
    return pltpu.CompilerParams(
        collective_id=cid, has_side_effects=True, vmem_limit_bytes=VLIM
    )


def place():
    s = lax.axis_index("site")
    b = lax.axis_index("bond")
    return s, b // 4, (b // 2) % 2, b % 2


def bond(x, y, c):
    return (x * 2 + y) * 2 + c


def greet(sends_to_me, count):
    barrier = pltpu.get_barrier_semaphore()
    for dev in sends_to_me:
        pl.semaphore_signal(barrier, inc=1, device_id=dev, device_id_type=MESH)
    pl.semaphore_wait(barrier, count)


def rcopy(src, dst, ssem, rsem, dev):
    return pltpu.make_async_remote_copy(
        src_ref=src, dst_ref=dst, send_sem=ssem, recv_sem=rsem,
        device_id=dev, device_id_type=MESH,
    )


def gather_kernel(own, out, zs, zr, ys, yr, xs, xr, cs, cr):
    s, x, y, c = place()
    xp, xm = (x + 1) % 4, (x + 3) % 4
    x2 = (x + 2) % 4
    yn = 1 - y
    seam_in = (s % 8) // 7
    seam_out = ((s + 7) % 8) // 7
    h = (y + seam_in) % 2
    hn = 1 - h
    sl, sr = (s + 15) % 16, (s + 1) % 16
    to_left = (sl, bond(x, (y + seam_out) % 2, c))
    from_right = (sr, bond(x, h, c))
    y_dev = (s, bond(x, yn, c))
    xp_dev = (s, bond(xp, y, c))
    xm_dev = (s, bond(xm, y, c))
    c_dev = (s, bond(x, y, 1 - c))
    greet((from_right, y_dev, xp_dev, xm_dev, c_dev), 5)

    def slot(cc, xx, yy, k):
        return out.at[cc * 8 + xx * 2 + yy, pl.ds(16 * k, 16)]

    started = []

    def send(src, dst, ss, rs, dev):
        d = rcopy(src, dst, ss, rs, dev)
        d.start()
        started.append(d)
        return d

    n_core = [0]

    def to_core(xx, yy, k):
        i = n_core[0]
        n_core[0] += 1
        return send(slot(c, xx, yy, k), slot(c, xx, yy, k), cs.at[i], cr.at[i], c_dev)

    z = [
        send(own.at[pl.ds(16 * k, 16)], slot(c, x, y, k), zs.at[k], zr.at[k], to_left)
        for k in range(2)
    ]
    ysend, xsend, core = [], [], []
    for k in range(2):
        z[k].wait_recv()
        ysend.append(send(slot(c, x, h, k), slot(c, x, h, k), ys.at[k], yr.at[k], y_dev))
        for i, dev in enumerate((xp_dev, xm_dev)):
            send(slot(c, x, h, k), slot(c, x, h, k), xs.at[i, 0, k], xr.at[i, 0, k], dev)
        core.append(to_core(x, h, k))

    def arrived(i, j, k, xx, yy):
        pltpu.make_async_copy(slot(c, xx, yy, k), slot(c, xx, yy, k), xr.at[i, j, k]).wait()

    for k in range(2):
        ysend[k].wait_recv()
        for i, dev in enumerate((xp_dev, xm_dev)):
            send(slot(c, x, hn, k), slot(c, x, hn, k), xs.at[i, 1, k], xr.at[i, 1, k], dev)
        core.append(to_core(x, hn, k))
    for j, yy in ((0, h), (1, hn)):
        for k in range(2):
            arrived(0, j, k, xm, yy)
            if k == 0:
                send(slot(c, xm, yy, 0), slot(c, xm, yy, 0), xs.at[0, 2, j], xr.at[0, 2, j], xp_dev)
            core.append(to_core(xm, yy, k))
            arrived(1, j, k, xp, yy)
            if k == 1:
                send(slot(c, xp, yy, 1), slot(c, xp, yy, 1), xs.at[1, 2, j], xr.at[1, 2, j], xm_dev)
            core.append(to_core(xp, yy, k))
    for j, yy in ((0, h), (1, hn)):
        pltpu.make_async_copy(slot(c, x2, yy, 0), slot(c, x2, yy, 0), xr.at[0, 2, j]).wait()
        core.append(to_core(x2, yy, 0))
        pltpu.make_async_copy(slot(c, x2, yy, 1), slot(c, x2, yy, 1), xr.at[1, 2, j]).wait()
        core.append(to_core(x2, yy, 1))
    for d in core:
        d.wait_recv()
    for d in started:
        d.wait_send()


def gather(own, cid):
    sem = pltpu.SemaphoreType.DMA
    return pl.pallas_call(
        gather_kernel,
        name="gather%d" % cid,
        out_shape=jax.ShapeDtypeStruct((16, 32, PHYS * CHI), BF16),
        in_specs=[ANY],
        out_specs=ANY,
        scratch_shapes=[
            sem((2,)), sem((2,)), sem((2,)), sem((2,)),
            sem((2, 3, 2)), sem((2, 3, 2)), sem((16,)), sem((16,)),
        ],
        compiler_params=params(cid),
    )(own)


BLOCKS = [(0, 0), (1, 0), (1, 1), (2, 0), (2, 1), (2, 2), (3, 0), (3, 1), (3, 2), (3, 3)]


def theta_kernel(a, b, proj, gate3, theta, sketch, pay, raw):
    a_val = a[...]

    def raw_step(t, _):
        cols = pl.ds(pl.multiple_of(t * CHI, CHI), CHI)
        acc = None
        for c in range(2):
            part = jnp.concatenate(
                [b[(i % 2) * 8 + i // 2, :, cols] for i in range(8 * c, 8 * c + 8)], axis=0
            )
            term = jnp.dot(a_val[:, c * 256:(c + 1) * 256], part, preferred_element_type=F32)
            acc = term if acc is None else acc + term
        raw[:, cols] = acc
        return 0

    lax.fori_loop(0, PHYS, raw_step, 0)
    g3 = gate3[...]

    def gate_step(i, ss):
        halves = []
        for e in range(2):
            rows = pl.ds(pl.multiple_of(i * 16, 16) + 8 * e, 8)
            xr = jnp.concatenate(
                [raw[rows, t * CHI:(t + 1) * CHI] for t in range(PHYS)], axis=0
            )
            hi = xr.astype(BF16)
            lo = (xr - hi.astype(F32)).astype(BF16)
            x3 = jnp.concatenate([hi, lo, hi], axis=0)
            g = jnp.dot(g3, x3, preferred_element_type=F32)
            for v in range(PHYS):
                gv = g[v * 8:(v + 1) * 8, :]
                ss = ss + gv * gv
            halves.append(g)
        rows = pl.ds(pl.multiple_of(i * 16, 16), 16)
        for v in range(PHYS):
            pair = jnp.concatenate([h[v * 8:(v + 1) * 8, :] for h in halves], axis=0)
            theta[rows, v * CHI:(v + 1) * CHI] = pair.astype(BF16)
        return ss

    ss = lax.fori_loop(0, 16, gate_step, jnp.zeros((8, CHI), F32))
    ss = (ss[:, 0:128] + ss[:, 128:256]) + (ss[:, 256:384] + ss[:, 384:512])
    sk = jnp.dot(theta[...], proj[...], preferred_element_type=F32)
    sketch[...] = sk
    skt = sk.T
    for n, (bi, bj) in enumerate(BLOCKS):
        blk = lax.dot_general(
            skt[bi * 128:(bi + 1) * 128, :], sk[:, bj * 128:(bj + 1) * 128],
            (((1,), (0,)), ((), ())), precision=HI, preferred_element_type=F32,
        )
        r = 128 * n
        while r < 128 * n + 128:
            p, o = r // 80, r % 80
            e = min(80 - o, 128 * n + 128 - r)
            pay[p, o:o + e, :] = blk[r - 128 * n:r - 128 * n + e, :]
            r += e
    for p in range(16):
        pay[p, 80:88, :] = ss


def theta_call(a, b, proj, gate3):
    return pl.pallas_call(
        theta_kernel,
        name="theta",
        out_shape=[
            jax.ShapeDtypeStruct((256, PHYS * CHI), BF16),
            jax.ShapeDtypeStruct((256, CHI), F32),
            jax.ShapeDtypeStruct((16, 88, 128), F32),
        ],
        in_specs=[VMEM] * 4,
        out_specs=[VMEM] * 3,
        scratch_shapes=[pltpu.VMEM((256, PHYS * CHI), F32)],
        compiler_params=params(),
    )(a, b, proj, gate3)


def gram_kernel(pay, out, half, rb0, rb1, s0, r0, s1, r1, s2, r2, s3, r3):
    s, x, y, c = place()
    me = x * 2 + y
    c_dev = (s, bond(x, y, 1 - c))
    peers = []
    for k in range(1, 8):
        q = (me + k) % 8
        peers.append((k, q, (s, bond(q // 2, q % 2, c))))
    greet([c_dev] + [p[2] for p in peers], 8)

    first = rcopy(pay.at[pl.ds((1 - c) * 8, 8)], rb0, s0, r0, c_dev)
    first.start()
    first.wait_recv()
    half[...] = pay[pl.ds(c * 8, 8)] + rb0[...]
    sends = [first]
    recvs = []
    for k, q, dev in peers:
        d = rcopy(half.at[q], rb1.at[k - 1], s1.at[k - 1], r1.at[k - 1], dev)
        d.start()
        sends.append(d)
        recvs.append(d)
    acc = half[me]
    for d in recvs:
        d.wait_recv()
    t = [rb1[k] for k in range(7)]
    mine = ((acc + t[0]) + (t[1] + t[2])) + ((t[3] + t[4]) + (t[5] + t[6]))
    slot = c * 8 + me
    out[slot] = mine
    bcast = []
    for k, q, dev in peers:
        d = rcopy(out.at[slot], out.at[slot], s2.at[k - 1], r2.at[k - 1], dev)
        d.start()
        sends.append(d)
        bcast.append(d)
    core = []
    d = rcopy(out.at[slot], out.at[slot], s3.at[0], r3.at[0], c_dev)
    d.start()
    core.append(d)
    for k in range(1, 8):
        bcast[k - 1].wait_recv()
        src = c * 8 + (me + 8 - k) % 8
        d = rcopy(out.at[src], out.at[src], s3.at[k], r3.at[k], c_dev)
        d.start()
        core.append(d)
    for d in core:
        d.wait_recv()
    for d in sends + core:
        d.wait_send()


def gram_call(pay, cid):
    sem = pltpu.SemaphoreType.DMA
    return pl.pallas_call(
        gram_kernel,
        name="gram%d" % cid,
        out_shape=jax.ShapeDtypeStruct((16, 88, 128), F32),
        in_specs=[VMEM],
        out_specs=VMEM,
        scratch_shapes=[
            pltpu.VMEM((8, 88, 128), F32), pltpu.VMEM((8, 88, 128), F32),
            pltpu.VMEM((7, 88, 128), F32),
            sem, sem, sem((7,)), sem((7,)), sem((7,)), sem((7,)), sem((8,)), sem((8,)),
        ],
        compiler_params=params(cid),
    )(pay)


def bl(v, k):
    return jnp.broadcast_to(v[:, k:k + 1], (8, 128))


def bs(v, j):
    return jnp.broadcast_to(v[j:j + 1, :], (8, 128))


def leaf(rows):
    lane = lax.broadcasted_iota(jnp.int32, (8, 128), 1)
    sub = lax.broadcasted_iota(jnp.int32, (8, 128), 0)
    rows = list(rows)
    out = []
    n = len(rows)
    for p in range(n):
        m_p = rows[p]
        c = [bl(m_p, 8 * p + v) for v in range(8)]
        pc = (lane >= 8 * p) & (lane < 8 * p + 8)
        m_p = jnp.where(pc, jnp.where(lane - 8 * p == sub, 1.0, 0.0), m_p)
        fwd = m_p
        diag = None
        for j in range(8):
            d = bs(c[j], j)
            isj = sub == j
            mult = jnp.where(isj, 0.0, c[j] * (1.0 / d))
            if j:
                diag = jnp.where(isj, d, diag)
                fwd = jnp.where(isj, m_p, fwd)
            else:
                diag = d
            for v in range(j + 1, 8):
                c[v] = c[v] - mult * bs(c[v], j)
            m_p = m_p - mult * bs(m_p, j)
        out.append(jnp.where(lane < 8 * p + 8, fwd * lax.rsqrt(diag), 0.0))
        if p == n - 1:
            break
        yy = m_p * (1.0 / diag)
        yb = [bs(yy, v) for v in range(8)]
        for q in range(p + 1, n):
            t = [bl(rows[q], 8 * p + v) * yb[v] for v in range(8)]
            tot = ((t[0] + t[1]) + (t[2] + t[3])) + ((t[4] + t[5]) + (t[6] + t[7]))
            rows[q] = jnp.where(pc, 0.0, rows[q]) - tot
    return out


def dott(a, b):
    return lax.dot_general(
        a, b, (((1,), (1,)), ((), ())), precision=HI, preferred_element_type=F32
    )


def dotn(a, b):
    return lax.dot_general(
        a, b, (((1,), (0,)), ((), ())), precision=HI, preferred_element_type=F32
    )


def chol_body(a, linv):
    linv[...] = jnp.zeros_like(linv)
    for b in range(4):
        o = b * 128
        x = jnp.concatenate(leaf([a[o + 8 * q:o + 8 * q + 8, o:o + 128] for q in range(16)]), 0)
        linv[o:o + 128, o:o + 128] = x
        if b < 3:
            lb = dott(a[o + 128:, o:o + 128], x)
            a[o + 128:, o:o + 128] = lb
            a[o + 128:, o + 128:] = a[o + 128:, o + 128:] - dott(lb, lb)
        if b > 0:
            t = dotn(a[o:o + 128, :o], linv[:o, :o])
            linv[o:o + 128, :o] = -dotn(x, t)


def chol_kernel(pay, sketch, theta, left, part, log, a, linv, leftf):
    for n, (bi, bj) in enumerate(BLOCKS):
        r = 128 * n
        while r < 128 * n + 128:
            p, o = r // 80, r % 80
            e = min(80 - o, 128 * n + 128 - r)
            q = bi * 128 + r - 128 * n
            a[q:q + e, bj * 128:(bj + 1) * 128] = pay[p, o:o + e, :]
            r += e
    chol_body(a, linv)
    root = math.sqrt(PHYS * CHI)
    ln = (dott(sketch[...], linv[...]) * root).astype(BF16)
    left[...] = ln
    leftf[...] = ln.astype(F32).T.astype(BF16)
    total = jnp.sum(jnp.sum(pay[0, 80:88, :], axis=0, keepdims=True), axis=1, keepdims=True)
    mean_square = total * (1.0 / (CHI * PHYS * PHYS * CHI)) + epsilon
    log[...] = jnp.broadcast_to(0.5 * jnp.log(mean_square), (8, 128))
    scale = lax.rsqrt(mean_square) * (1.0 / root)

    def step(t, _):
        cols = pl.ds(pl.multiple_of(t * CHI, CHI), CHI)
        blk = jnp.dot(leftf[...], theta[:, cols], preferred_element_type=F32)
        blk = (blk * scale).astype(BF16)
        for xx in range(4):
            for y in range(2):
                for cc in range(2):
                    b = (xx * 2 + y) * 2 + cc
                    part[cc * 8 + xx * 2 + y, :, cols] = blk[b * 32:(b + 1) * 32, :]
        return 0

    lax.fori_loop(0, PHYS, step, 0)


def chol_call(pay, sketch, theta):
    return pl.pallas_call(
        chol_kernel,
        name="chol",
        out_shape=[
            jax.ShapeDtypeStruct((256, CHI), BF16),
            jax.ShapeDtypeStruct((16, 32, PHYS * CHI), BF16),
            jax.ShapeDtypeStruct((8, 128), F32),
        ],
        in_specs=[VMEM] * 3,
        out_specs=[VMEM] * 3,
        scratch_shapes=[
            pltpu.VMEM((CHI, CHI), F32), pltpu.VMEM((CHI, CHI), F32), pltpu.VMEM((CHI, 256), BF16),
        ],
        compiler_params=params(),
    )(pay, sketch, theta)


def add16(dst, di, src, si, rows):
    def step(t, _):
        cols = pl.ds(pl.multiple_of(t * CHI, CHI), CHI)
        v = dst[di, rows, cols].astype(F32) + src[si, rows, cols].astype(F32)
        dst[di, rows, cols] = v.astype(BF16)
        return 0

    lax.fori_loop(0, PHYS, step, 0)


def scatter_kernel(part, out, fin, rbc, rbd, rbx, rby,
                   cs, cr, ds, dr, xs, xr, ys, yr, zs, zr):
    s, x, y, c = place()
    xp, xm, x2 = (x + 1) % 4, (x + 3) % 4, (x + 2) % 4
    yn = 1 - y
    seam_out = (s % 8) // 7
    seam_in = ((s + 7) % 8) // 7
    h = (y + seam_out) % 2
    hn = 1 - h
    to_right = ((s + 1) % 16, bond(x, h, c))
    from_left = ((s + 15) % 16, bond(x, (y + seam_in) % 2, c))
    y_dev = (s, bond(x, yn, c))
    xp_dev = (s, bond(xp, y, c))
    xm_dev = (s, bond(xm, y, c))
    c_dev = (s, bond(x, y, 1 - c))
    greet((from_left, y_dev, xp_dev, xm_dev, c_dev), 5)
    sends = []

    def send(src, dst, ss, rs, dev):
        d = rcopy(src, dst, ss, rs, dev)
        d.start()
        sends.append(d)
        return d

    full = pl.ds(0, 32)
    lo, hi = pl.ds(0, 16), pl.ds(16, 16)
    order = ((x2, 0), (x2, 1), (xp, 0), (xp, 1), (xm, 0), (xm, 1), (x, 0), (x, 1))
    core = []
    for i, (xx, j) in enumerate(order):
        yy = h if j == 0 else hn
        sl = xx * 2 + yy
        core.append(send(part.at[(1 - c) * 8 + sl], rbc.at[i], cs.at[i], cr.at[i], c_dev))
    dist = []
    for i in range(2):
        yy = h if i == 0 else hn
        core[i].wait_recv()
        sl = c * 8 + x2 * 2 + yy
        add16(part, sl, rbc, i, full)
        dist.append((
            send(part.at[sl, lo], rbd.at[0, i], ds.at[0, i], dr.at[0, i], xp_dev),
            send(part.at[sl, hi], rbd.at[1, i], ds.at[1, i], dr.at[1, i], xm_dev),
        ))
    near = []
    for i in range(2):
        yy = h if i == 0 else hn
        for w, (xx, dev, rows) in enumerate(((xp, xp_dev, lo), (xm, xm_dev, hi))):
            n = 2 + 2 * w + i
            core[n].wait_recv()
            sl = c * 8 + xx * 2 + yy
            add16(part, sl, rbc, n, full)
            dist[i][w].wait_recv()

            def step(t, _, sl=sl, w=w, i=i, rows=rows):
                cols = pl.ds(pl.multiple_of(t * CHI, CHI), CHI)
                v = part[sl, rows, cols].astype(F32) + rbd[w, i, :, cols].astype(F32)
                part[sl, rows, cols] = v.astype(BF16)
                return 0

            lax.fori_loop(0, PHYS, step, 0)
            near.append(send(part.at[sl], rbx.at[w, i], xs.at[w, i], xr.at[w, i], dev))
    for j, yy in ((1, hn), (0, h)):
        n = 6 + j
        core[n].wait_recv()
        sl = c * 8 + x * 2 + yy
        near[2 * j].wait_recv()
        near[2 * j + 1].wait_recv()

        def step3(t, _, sl=sl, n=n, j=j):
            cols = pl.ds(pl.multiple_of(t * CHI, CHI), CHI)
            v = (part[sl, :, cols].astype(F32) + rbc[n, :, cols].astype(F32)) + (
                rbx[0, j, :, cols].astype(F32) + rbx[1, j, :, cols].astype(F32))
            part[sl, :, cols] = v.astype(BF16)
            return 0

        lax.fori_loop(0, PHYS, step3, 0)
        if j == 1:
            ysend = send(part.at[sl], rby, ys, yr, y_dev)
    ysend.wait_recv()
    sl = c * 8 + x * 2 + h

    def step4(t, _):
        cols = pl.ds(pl.multiple_of(t * CHI, CHI), CHI)
        v = part[sl, :, cols].astype(F32) + rby[:, cols].astype(F32)
        fin[:, cols] = v.astype(BF16)
        return 0

    lax.fori_loop(0, PHYS, step4, 0)
    z = send(fin, out, zs, zr, to_right)
    z.wait_recv()
    for d in sends:
        d.wait_send()


def scatter_call(part, cid):
    sem = pltpu.SemaphoreType.DMA
    wide = PHYS * CHI

    def body(part_in, out, part_v, *rest):
        pltpu.sync_copy(part_in, part_v)
        scatter_kernel(part_v, out, *rest)

    return pl.pallas_call(
        body,
        name="scatter%d" % cid,
        out_shape=jax.ShapeDtypeStruct((32, wide), BF16),
        in_specs=[ANY],
        out_specs=VMEM,
        scratch_shapes=[
            pltpu.VMEM((16, 32, wide), BF16),
            pltpu.VMEM((32, wide), BF16), pltpu.VMEM((8, 32, wide), BF16),
            pltpu.VMEM((2, 2, 16, wide), BF16), pltpu.VMEM((2, 2, 32, wide), BF16),
            pltpu.VMEM((32, wide), BF16),
            sem((8,)), sem((8,)), sem((2, 2)), sem((2, 2)), sem((2, 2)), sem((2, 2)),
            sem, sem, sem, sem,
        ],
        compiler_params=params(cid),
    )(part)


def gate_split(gates, position):
    g = lax.dynamic_index_in_dim(gates, position, 0, keepdims=False)
    g = g.reshape(8, 8, 8, 8).transpose(1, 0, 3, 2).reshape(64, 64)
    hi = lax.reduce_precision(g, 8, 7)
    lo = (g - hi).astype(BF16)
    hi = hi.astype(BF16)
    return jnp.concatenate([hi, hi, lo], axis=1)


def shards(mps, projection, gates):
    position = lax.axis_index("site")
    state = mps[0]
    gate3 = gate_split(gates, position)
    proj = projection[0]
    log_out = jnp.zeros((1,), F32)
    for parity in range(2):
        is_left = position % 2 == parity
        b = gather(state.reshape(32, PHYS * CHI), 3 * parity)
        theta, sketch, pay = theta_call(state.reshape(256, CHI), b, proj, gate3)
        pay = gram_call(pay, 3 * parity + 1)
        left, part, log = chol_call(pay, sketch, theta)
        right = scatter_call(part, 3 * parity + 2)
        state = jnp.where(
            is_left, left.reshape(32, PHYS, CHI), right.reshape(32, PHYS, CHI)
        )
        log_out = jnp.where(is_left, log[0, 0:1], log_out)
    return state[None], log_out


def solution(mesh):
    return jax.shard_map(
        shards,
        mesh=mesh,
        in_specs=(P("site", "bond", None, None), P("site", None, None), P()),
        out_specs=(P("site", "bond", None, None), P("site")),
        check_vma=False,
    )
```

```python
import functools
import math

import jax
import jax.numpy as jnp
from jax import lax
from jax.experimental import pallas as pl
from jax.experimental.pallas import tpu as pltpu
from jax.sharding import PartitionSpec as P

PHYS = 8
CHI = 512
epsilon = 1e-06
MESH = pl.DeviceIdType.MESH
HI = lax.Precision.HIGHEST
F32 = jnp.float32
BF16 = jnp.bfloat16
VMEM = pl.BlockSpec(memory_space=pltpu.VMEM)
ANY = pl.BlockSpec(memory_space=pl.ANY)
VLIM = 56 << 20


def params(cid=None):
    if cid is None:
        return pltpu.CompilerParams(vmem_limit_bytes=VLIM)
    return pltpu.CompilerParams(
        collective_id=cid, has_side_effects=True, vmem_limit_bytes=VLIM
    )


def place():
    s = lax.axis_index("site")
    b = lax.axis_index("bond")
    return s, b // 4, (b // 2) % 2, b % 2


def bond(x, y, c):
    return (x * 2 + y) * 2 + c


def greet(sends_to_me, count):
    barrier = pltpu.get_barrier_semaphore()
    for dev in sends_to_me:
        pl.semaphore_signal(barrier, inc=1, device_id=dev, device_id_type=MESH)
    pl.semaphore_wait(barrier, count)


def rcopy(src, dst, ssem, rsem, dev):
    return pltpu.make_async_remote_copy(
        src_ref=src, dst_ref=dst, send_sem=ssem, recv_sem=rsem,
        device_id=dev, device_id_type=MESH,
    )


class Ring:
    def __init__(self, out, sems, s, x, y, c, h):
        self.out, self.c = out, c
        self.ys, self.yr, self.xs, self.xr, self.cs, self.cr = sems
        self.x, self.h = x, h
        self.xp, self.xm, self.x2 = (x + 1) % 4, (x + 3) % 4, (x + 2) % 4
        self.hn = 1 - h
        self.y_dev = (s, bond(x, 1 - y, c))
        self.xp_dev = (s, bond(self.xp, y, c))
        self.xm_dev = (s, bond(self.xm, y, c))
        self.c_dev = (s, bond(x, y, 1 - c))
        self.partners = [self.y_dev, self.xp_dev, self.xm_dev, self.c_dev]
        self.started, self.core, self.ysend = [], [], []

    def slot(self, xx, yy, k):
        return self.out.at[self.c * 8 + xx * 2 + yy, pl.ds(128 * k, 128)]

    def send(self, ref, ss, rs, dev):
        d = rcopy(ref, ref, ss, rs, dev)
        d.start()
        self.started.append(d)
        return d

    def to_core(self, xx, yy, k):
        i = len(self.core)
        ref = self.slot(xx, yy, k)
        self.core.append(self.send(ref, self.cs.at[i], self.cr.at[i], self.c_dev))

    def home(self, k):
        ref = self.slot(self.x, self.h, k)
        self.ysend.append(self.send(ref, self.ys.at[k], self.yr.at[k], self.y_dev))
        for i, dev in enumerate((self.xp_dev, self.xm_dev)):
            self.send(ref, self.xs.at[i, 0, k], self.xr.at[i, 0, k], dev)
        self.to_core(self.x, self.h, k)

    def arrived(self, i, j, k, xx, yy, part):
        ref = self.slot(xx, yy, part)
        pltpu.make_async_copy(ref, ref, self.xr.at[i, j, k]).wait()

    def rest(self):
        x, h, hn, xp, xm, x2 = self.x, self.h, self.hn, self.xp, self.xm, self.x2
        xs, xr = self.xs, self.xr
        for k in range(2):
            self.ysend[k].wait_recv()
            for i, dev in enumerate((self.xp_dev, self.xm_dev)):
                self.send(self.slot(x, hn, k), xs.at[i, 1, k], xr.at[i, 1, k], dev)
            self.to_core(x, hn, k)
        for j, yy in ((0, h), (1, hn)):
            for k in range(2):
                self.arrived(0, j, k, xm, yy, k)
                if k == 0:
                    self.send(self.slot(xm, yy, 0), xs.at[0, 2, j], xr.at[0, 2, j], self.xp_dev)
                self.to_core(xm, yy, k)
                self.arrived(1, j, k, xp, yy, k)
                if k == 1:
                    self.send(self.slot(xp, yy, 1), xs.at[1, 2, j], xr.at[1, 2, j], self.xm_dev)
                self.to_core(xp, yy, k)
        for j, yy in ((0, h), (1, hn)):
            self.arrived(0, 2, j, x2, yy, 0)
            self.to_core(x2, yy, 0)
            self.arrived(1, 2, j, x2, yy, 1)
            self.to_core(x2, yy, 1)
        for d in self.core:
            d.wait_recv()

    def drain(self):
        for d in self.started:
            d.wait_send()


def ring_sems():
    sem = pltpu.SemaphoreType.DMA
    return [sem((2,)), sem((2,)), sem((2, 3, 2)), sem((2, 3, 2)), sem((16,)), sem((16,))]


def seams(s, x, y, c):
    h = (y + (s % 8) // 7) % 2
    to_left = ((s + 15) % 16, bond(x, (y + ((s + 7) % 8) // 7) % 2, c))
    from_right = ((s + 1) % 16, bond(x, h, c))
    return h, to_left, from_right


def gather_kernel(own, out, zs, zr, *sems):
    s, x, y, c = place()
    h, to_left, from_right = seams(s, x, y, c)
    ring = Ring(out, sems, s, x, y, c, h)
    greet([from_right] + ring.partners, 5)
    z = []
    for k in range(2):
        d = rcopy(
            own.at[pl.ds(128 * k, 128)], out.at[c * 8 + x * 2 + y, pl.ds(128 * k, 128)],
            zs.at[k], zr.at[k], to_left,
        )
        d.start()
        z.append(d)
    for k in range(2):
        z[k].wait_recv()
        ring.home(k)
    ring.rest()
    for d in z:
        d.wait_send()
    ring.drain()


def gather(own, cid):
    sem = pltpu.SemaphoreType.DMA
    return pl.pallas_call(
        gather_kernel,
        name="gather%d" % cid,
        out_shape=jax.ShapeDtypeStruct((16, 256, CHI), BF16),
        in_specs=[ANY],
        out_specs=ANY,
        scratch_shapes=[sem((2,)), sem((2,))] + ring_sems(),
        compiler_params=params(cid),
    )(own)


BLOCKS = [(0, 0), (1, 0), (1, 1), (2, 0), (2, 1), (2, 2), (3, 0), (3, 1), (3, 2), (3, 3)]


def theta_kernel(a, b, proj, gate3, theta, sketch, pay, raw):
    a_val = a[...]

    def raw_step(t, _):
        cols = pl.ds(pl.multiple_of(t * CHI, CHI), CHI)
        rows = pl.ds(pl.multiple_of(t * 32, 32), 32)
        acc = None
        for c in range(2):
            part = jnp.concatenate(
                [b[(i % 2) * 8 + i // 2, rows, :] for i in range(8 * c, 8 * c + 8)], axis=0
            )
            term = jnp.dot(a_val[:, c * 256:(c + 1) * 256], part, preferred_element_type=F32)
            acc = term if acc is None else acc + term
        raw[:, cols] = acc
        return 0

    lax.fori_loop(0, PHYS, raw_step, 0)
    g3 = gate3[...]

    def gate_step(i, ss):
        halves = []
        for e in range(2):
            rows = pl.ds(pl.multiple_of(i * 16, 16) + 8 * e, 8)
            xr = jnp.concatenate(
                [raw[rows, t * CHI:(t + 1) * CHI] for t in range(PHYS)], axis=0
            )
            hi = xr.astype(BF16)
            lo = (xr - hi.astype(F32)).astype(BF16)
            x3 = jnp.concatenate([hi, lo, hi], axis=0)
            g = jnp.dot(g3, x3, preferred_element_type=F32)
            for v in range(PHYS):
                gv = g[v * 8:(v + 1) * 8, :]
                ss = ss + gv * gv
            halves.append(g)
        rows = pl.ds(pl.multiple_of(i * 16, 16), 16)
        for v in range(PHYS):
            pair = jnp.concatenate([h[v * 8:(v + 1) * 8, :] for h in halves], axis=0)
            theta[rows, v * CHI:(v + 1) * CHI] = pair.astype(BF16)
        return ss

    ss = lax.fori_loop(0, 16, gate_step, jnp.zeros((8, CHI), F32))
    ss = (ss[:, 0:128] + ss[:, 128:256]) + (ss[:, 256:384] + ss[:, 384:512])
    sk = jnp.dot(theta[...], proj[...], preferred_element_type=F32)
    sketch[...] = sk
    skt = sk.T
    for n, (bi, bj) in enumerate(BLOCKS):
        blk = lax.dot_general(
            skt[bi * 128:(bi + 1) * 128, :], sk[:, bj * 128:(bj + 1) * 128],
            (((1,), (0,)), ((), ())), precision=HI, preferred_element_type=F32,
        )
        r = 128 * n
        while r < 128 * n + 128:
            p, o = r // 80, r % 80
            e = min(80 - o, 128 * n + 128 - r)
            pay[p, o:o + e, :] = blk[r - 128 * n:r - 128 * n + e, :]
            r += e
    for p in range(16):
        pay[p, 80:88, :] = ss


def theta_call(a, b, proj, gate3):
    return pl.pallas_call(
        theta_kernel,
        name="theta",
        out_shape=[
            jax.ShapeDtypeStruct((256, PHYS * CHI), BF16),
            jax.ShapeDtypeStruct((256, CHI), F32),
            jax.ShapeDtypeStruct((16, 88, 128), F32),
        ],
        in_specs=[VMEM] * 4,
        out_specs=[VMEM] * 3,
        scratch_shapes=[pltpu.VMEM((256, PHYS * CHI), F32)],
        compiler_params=params(),
    )(a, b, proj, gate3)


def gram_kernel(pay, out, half, rb0, rb1, s0, r0, s1, r1, s2, r2, s3, r3):
    s, x, y, c = place()
    me = x * 2 + y
    c_dev = (s, bond(x, y, 1 - c))
    peers = []
    for k in range(1, 8):
        q = (me + k) % 8
        peers.append((k, q, (s, bond(q // 2, q % 2, c))))
    greet([c_dev] + [p[2] for p in peers], 8)

    first = rcopy(pay.at[pl.ds((1 - c) * 8, 8)], rb0, s0, r0, c_dev)
    first.start()
    first.wait_recv()
    half[...] = pay[pl.ds(c * 8, 8)] + rb0[...]
    sends = [first]
    recvs = []
    for k, q, dev in peers:
        d = rcopy(half.at[q], rb1.at[k - 1], s1.at[k - 1], r1.at[k - 1], dev)
        d.start()
        sends.append(d)
        recvs.append(d)
    acc = half[me]
    for d in recvs:
        d.wait_recv()
    t = [rb1[k] for k in range(7)]
    mine = ((acc + t[0]) + (t[1] + t[2])) + ((t[3] + t[4]) + (t[5] + t[6]))
    slot = c * 8 + me
    out[slot] = mine
    bcast = []
    for k, q, dev in peers:
        d = rcopy(out.at[slot], out.at[slot], s2.at[k - 1], r2.at[k - 1], dev)
        d.start()
        sends.append(d)
        bcast.append(d)
    core = []
    d = rcopy(out.at[slot], out.at[slot], s3.at[0], r3.at[0], c_dev)
    d.start()
    core.append(d)
    for k in range(1, 8):
        bcast[k - 1].wait_recv()
        src = c * 8 + (me + 8 - k) % 8
        d = rcopy(out.at[src], out.at[src], s3.at[k], r3.at[k], c_dev)
        d.start()
        core.append(d)
    for d in core:
        d.wait_recv()
    for d in sends + core:
        d.wait_send()


def gram_call(pay, cid):
    sem = pltpu.SemaphoreType.DMA
    return pl.pallas_call(
        gram_kernel,
        name="gram%d" % cid,
        out_shape=jax.ShapeDtypeStruct((16, 88, 128), F32),
        in_specs=[VMEM],
        out_specs=VMEM,
        scratch_shapes=[
            pltpu.VMEM((8, 88, 128), F32), pltpu.VMEM((8, 88, 128), F32),
            pltpu.VMEM((7, 88, 128), F32),
            sem, sem, sem((7,)), sem((7,)), sem((7,)), sem((7,)), sem((8,)), sem((8,)),
        ],
        compiler_params=params(cid),
    )(pay)


def bl(v, k):
    return jnp.broadcast_to(v[:, k:k + 1], (8, 128))


def bs(v, j):
    return jnp.broadcast_to(v[j:j + 1, :], (8, 128))


def leaf(rows):
    lane = lax.broadcasted_iota(jnp.int32, (8, 128), 1)
    sub = lax.broadcasted_iota(jnp.int32, (8, 128), 0)
    rows = list(rows)
    out = []
    n = len(rows)
    for p in range(n):
        m_p = rows[p]
        c = [bl(m_p, 8 * p + v) for v in range(8)]
        pc = (lane >= 8 * p) & (lane < 8 * p + 8)
        m_p = jnp.where(pc, jnp.where(lane - 8 * p == sub, 1.0, 0.0), m_p)
        fwd = m_p
        diag = None
        for j in range(8):
            d = bs(c[j], j)
            isj = sub == j
            mult = jnp.where(isj, 0.0, c[j] * (1.0 / d))
            if j:
                diag = jnp.where(isj, d, diag)
                fwd = jnp.where(isj, m_p, fwd)
            else:
                diag = d
            for v in range(j + 1, 8):
                c[v] = c[v] - mult * bs(c[v], j)
            m_p = m_p - mult * bs(m_p, j)
        out.append(jnp.where(lane < 8 * p + 8, fwd * lax.rsqrt(diag), 0.0))
        if p == n - 1:
            break
        yy = m_p * (1.0 / diag)
        yb = [bs(yy, v) for v in range(8)]
        for q in range(p + 1, n):
            t = [bl(rows[q], 8 * p + v) * yb[v] for v in range(8)]
            tot = ((t[0] + t[1]) + (t[2] + t[3])) + ((t[4] + t[5]) + (t[6] + t[7]))
            rows[q] = jnp.where(pc, 0.0, rows[q]) - tot
    return out


def dott(a, b):
    return lax.dot_general(
        a, b, (((1,), (1,)), ((), ())), precision=HI, preferred_element_type=F32
    )


def dotn(a, b):
    return lax.dot_general(
        a, b, (((1,), (0,)), ((), ())), precision=HI, preferred_element_type=F32
    )


def chol_body(a, linv):
    linv[...] = jnp.zeros_like(linv)
    for b in range(4):
        o = b * 128
        x = jnp.concatenate(leaf([a[o + 8 * q:o + 8 * q + 8, o:o + 128] for q in range(16)]), 0)
        linv[o:o + 128, o:o + 128] = x
        if b < 3:
            lb = dott(a[o + 128:, o:o + 128], x)
            a[o + 128:, o:o + 128] = lb
            a[o + 128:, o + 128:] = a[o + 128:, o + 128:] - dott(lb, lb)
        if b > 0:
            t = dotn(a[o:o + 128, :o], linv[:o, :o])
            linv[o:o + 128, :o] = -dotn(x, t)


def chol_kernel(pay, sketch, theta, left, leftp, thc, log, a, linv, ss, rs, own_sem):
    s, x, y, c = place()
    b = bond(x, y, c)
    peers = []
    for k in range(1, 16):
        q = (b + k) % 16
        peers.append((q, (s, q)))
    greet([p[1] for p in peers], 15)
    slot = c * 8 + x * 2 + y

    def columns(q):
        return theta.at[:, pl.ds(pl.multiple_of(q * 256, 256), 256)]

    own = pltpu.make_async_copy(columns(b), thc.at[slot], own_sem)
    own.start()
    moves = []
    for k, (q, dev) in enumerate(peers):
        d = rcopy(columns(q), thc.at[slot], ss.at[k], rs.at[k], dev)
        d.start()
        moves.append(d)
    for n, (bi, bj) in enumerate(BLOCKS):
        r = 128 * n
        while r < 128 * n + 128:
            p, o = r // 80, r % 80
            e = min(80 - o, 128 * n + 128 - r)
            q = bi * 128 + r - 128 * n
            a[q:q + e, bj * 128:(bj + 1) * 128] = pay[p, o:o + e, :]
            r += e
    chol_body(a, linv)
    root = math.sqrt(PHYS * CHI)
    ln = (dott(sketch[...], linv[...]) * root).astype(BF16)
    left[...] = ln
    ri = lax.broadcasted_iota(jnp.int32, (256, 256), 0)
    ci = lax.broadcasted_iota(jnp.int32, (256, 256), 1)
    perm = jnp.where(ci == (ri % 32) * 8 + ri // 32, 1.0, 0.0).astype(BF16)
    leftp[...] = jnp.dot(perm, ln, preferred_element_type=F32).astype(BF16)
    total = jnp.sum(jnp.sum(pay[0, 80:88, :], axis=0, keepdims=True), axis=1, keepdims=True)
    mean_square = total * (1.0 / (CHI * PHYS * PHYS * CHI)) + epsilon
    log[0:8, :] = jnp.broadcast_to(0.5 * jnp.log(mean_square), (8, 128))
    log[8:16, :] = jnp.broadcast_to(lax.rsqrt(mean_square) * (1.0 / root), (8, 128))
    own.wait()
    for d in moves:
        d.wait_recv()
    for d in moves:
        d.wait_send()


def chol_call(pay, sketch, theta, cid):
    sem = pltpu.SemaphoreType.DMA
    return pl.pallas_call(
        chol_kernel,
        name="chol%d" % cid,
        out_shape=[
            jax.ShapeDtypeStruct((256, CHI), BF16),
            jax.ShapeDtypeStruct((256, CHI), BF16),
            jax.ShapeDtypeStruct((16, 256, 256), BF16),
            jax.ShapeDtypeStruct((16, 128), F32),
        ],
        in_specs=[VMEM] * 3,
        out_specs=[VMEM] * 4,
        scratch_shapes=[
            pltpu.VMEM((CHI, CHI), F32), pltpu.VMEM((CHI, CHI), F32),
            sem((15,)), sem((15,)), sem,
        ],
        compiler_params=params(cid),
    )(pay, sketch, theta)


def tail_kernel(parity, last, left, leftp, thc, log, out, rcol, rsend, zs, zr, ls, as_, ar, *sems):
    s, x, y, c = place()
    is_left = s % 2 == parity
    h, to_left, from_right = seams(s, x, y, c)
    if last:
        h = y
    ring = Ring(out, sems, s, x, y, c, h)
    right, before = (s + 1) % 16, (s + 15) % 16
    targets = [(right, q) for q in range(16)]
    sources = [(before, q) for q in range(16)]
    greet(ring.partners + sources + ([] if last else [from_right]), 20 + (0 if last else 1))
    slot = c * 8 + x * 2 + y
    home = c * 8 + x * 2 + h

    def half(k):
        return pl.ds(128 * k, 128)

    if last:
        loc = [
            pltpu.make_async_copy(left.at[half(k)], out.at[slot, half(k)], ls.at[k])
            for k in range(2)
        ]
        for d in loc:
            d.start()
        for k in range(2):
            loc[k].wait()
            ring.home(k)
        ring.rest()
        ring.drain()
    else:
        loc = [
            pltpu.make_async_copy(left.at[half(k)], out.at[home, half(k)], ls.at[k])
            for k in range(2)
        ]
        z = [
            rcopy(leftp.at[half(k)], out.at[slot, half(k)], zs.at[k], zr.at[k], to_left)
            for k in range(2)
        ]

        @pl.when(is_left)
        def _():
            for k in range(2):
                loc[k].start()
                z[k].start()

        for k in range(2):
            @pl.when(is_left)
            def _():
                loc[k].wait()

            @pl.when(jnp.logical_not(is_left))
            def _():
                z[k].wait_recv()

            ring.home(k)
        ring.rest()

        @pl.when(is_left)
        def _():
            for k in range(2):
                z[k].wait_send()

        ring.drain()

    sends = [
        rcopy(rsend.at[q], rcol.at[bond(x, y, c)], as_.at[q], ar.at[bond(x, y, c)], targets[q])
        for q in range(16)
    ]

    @pl.when(is_left)
    def _():
        acc = lax.dot_general(
            out[...].reshape(4096, CHI), thc[...].reshape(4096, 256),
            (((0,), (0,)), ((), ())), preferred_element_type=F32,
        )
        blk = (acc * log[8:9, 0:1]).astype(BF16)
        for q in range(16):
            rsend[q] = blk[q * 32:(q + 1) * 32, :]
        for d in sends:
            d.start()
        for d in sends:
            d.wait_send()

    @pl.when(jnp.logical_not(is_left))
    def _():
        for q in range(16):
            pltpu.make_async_copy(rcol.at[q], rcol.at[q], ar.at[q]).wait()


def tail_call(left, leftp, thc, log, parity, cid):
    sem = pltpu.SemaphoreType.DMA
    return pl.pallas_call(
        functools.partial(tail_kernel, parity, parity == 1),
        name="tail%d" % cid,
        out_shape=[
            jax.ShapeDtypeStruct((16, 256, CHI), BF16),
            jax.ShapeDtypeStruct((16, 32, 256), BF16),
        ],
        in_specs=[VMEM] * 4,
        out_specs=[VMEM] * 2,
        scratch_shapes=[
            pltpu.VMEM((16, 32, 256), BF16),
            sem((2,)), sem((2,)), sem((2,)), sem((16,)), sem((16,)),
        ] + ring_sems(),
        compiler_params=params(cid),
    )(left, leftp, thc, log)


def gate_split(gates, position):
    g = lax.dynamic_index_in_dim(gates, position, 0, keepdims=False)
    g = g.reshape(8, 8, 8, 8).transpose(1, 0, 3, 2).reshape(64, 64)
    hi = lax.reduce_precision(g, 8, 7)
    lo = (g - hi).astype(BF16)
    hi = hi.astype(BF16)
    return jnp.concatenate([hi, hi, lo], axis=1)


def shards(mps, projection, gates):
    position = lax.axis_index("site")
    gate3 = gate_split(gates, position)
    proj = projection[0]
    b = gather(mps[0].transpose(1, 0, 2).reshape(256, CHI), 0)
    a = mps[0].reshape(256, CHI)
    logs, tensors = [], []
    for parity in range(2):
        theta, sketch, pay = theta_call(a, b, proj, gate3)
        pay = gram_call(pay, 3 * parity + 1)
        left, leftp, thc, log = chol_call(pay, sketch, theta, 3 * parity + 2)
        b, rcol = tail_call(left, leftp, thc, log, parity, 3 * parity + 3)
        a = rcol.reshape(PHYS, 2, 32, 256).transpose(2, 0, 1, 3).reshape(256, CHI)
        logs.append(log[0, 0:1])
        tensors.append(left)
    odd = position % 2 == 1
    state = jnp.where(odd, tensors[1], a).reshape(32, PHYS, CHI)
    return state[None], jnp.where(odd, logs[1], logs[0])


def solution(mesh):
    return jax.shard_map(
        shards,
        mesh=mesh,
        in_specs=(P("site", "bond", None, None), P("site", None, None), P()),
        out_specs=(P("site", "bond", None, None), P("site")),
        check_vma=False,
    )
```

```python
import functools
import math

import jax
import jax.numpy as jnp
from jax import lax
from jax.experimental import pallas as pl
from jax.experimental.pallas import tpu as pltpu
from jax.sharding import PartitionSpec as P

PHYS = 8
CHI = 512
epsilon = 1e-06
MESH = pl.DeviceIdType.MESH
HI = lax.Precision.HIGHEST
F32 = jnp.float32
BF16 = jnp.bfloat16
VMEM = pl.BlockSpec(memory_space=pltpu.VMEM)
ANY = pl.BlockSpec(memory_space=pl.ANY)
VLIM = 56 << 20


def params(cid=None):
    if cid is None:
        return pltpu.CompilerParams(vmem_limit_bytes=VLIM)
    return pltpu.CompilerParams(
        collective_id=cid, has_side_effects=True, vmem_limit_bytes=VLIM
    )


def place():
    s = lax.axis_index("site")
    b = lax.axis_index("bond")
    return s, b // 4, (b // 2) % 2, b % 2


def bond(x, y, c):
    return (x * 2 + y) * 2 + c


def greet(sends_to_me, count):
    barrier = pltpu.get_barrier_semaphore()
    for dev in sends_to_me:
        pl.semaphore_signal(barrier, inc=1, device_id=dev, device_id_type=MESH)
    pl.semaphore_wait(barrier, count)


def rcopy(src, dst, ssem, rsem, dev):
    return pltpu.make_async_remote_copy(
        src_ref=src, dst_ref=dst, send_sem=ssem, recv_sem=rsem,
        device_id=dev, device_id_type=MESH,
    )


class Ring:
    def __init__(self, out, sems, s, x, y, c, h):
        self.out, self.c = out, c
        self.ys, self.yr, self.xs, self.xr, self.cs, self.cr = sems
        self.x, self.h = x, h
        self.xp, self.xm, self.x2 = (x + 1) % 4, (x + 3) % 4, (x + 2) % 4
        self.hn = 1 - h
        self.y_dev = (s, bond(x, 1 - y, c))
        self.xp_dev = (s, bond(self.xp, y, c))
        self.xm_dev = (s, bond(self.xm, y, c))
        self.c_dev = (s, bond(x, y, 1 - c))
        self.partners = [self.y_dev, self.xp_dev, self.xm_dev, self.c_dev]
        self.started, self.core, self.ysend = [], [], []

    def slot(self, xx, yy, k):
        return self.out.at[self.c * 8 + xx * 2 + yy, pl.ds(128 * k, 128)]

    def send(self, ref, ss, rs, dev):
        d = rcopy(ref, ref, ss, rs, dev)
        d.start()
        self.started.append(d)
        return d

    def to_core(self, xx, yy, k):
        i = len(self.core)
        ref = self.slot(xx, yy, k)
        self.core.append(self.send(ref, self.cs.at[i], self.cr.at[i], self.c_dev))

    def home(self, k):
        ref = self.slot(self.x, self.h, k)
        self.ysend.append(self.send(ref, self.ys.at[k], self.yr.at[k], self.y_dev))
        for i, dev in enumerate((self.xp_dev, self.xm_dev)):
            self.send(ref, self.xs.at[i, 0, k], self.xr.at[i, 0, k], dev)
        self.to_core(self.x, self.h, k)

    def arrived(self, i, j, k, xx, yy, part):
        ref = self.slot(xx, yy, part)
        pltpu.make_async_copy(ref, ref, self.xr.at[i, j, k]).wait()

    def rest(self):
        x, h, hn, xp, xm, x2 = self.x, self.h, self.hn, self.xp, self.xm, self.x2
        xs, xr = self.xs, self.xr
        for k in range(2):
            self.ysend[k].wait_recv()
            for i, dev in enumerate((self.xp_dev, self.xm_dev)):
                self.send(self.slot(x, hn, k), xs.at[i, 1, k], xr.at[i, 1, k], dev)
            self.to_core(x, hn, k)
        for j, yy in ((0, h), (1, hn)):
            for k in range(2):
                self.arrived(0, j, k, xm, yy, k)
                if k == 0:
                    self.send(self.slot(xm, yy, 0), xs.at[0, 2, j], xr.at[0, 2, j], self.xp_dev)
                self.to_core(xm, yy, k)
                self.arrived(1, j, k, xp, yy, k)
                if k == 1:
                    self.send(self.slot(xp, yy, 1), xs.at[1, 2, j], xr.at[1, 2, j], self.xm_dev)
                self.to_core(xp, yy, k)
        for j, yy in ((0, h), (1, hn)):
            self.arrived(0, 2, j, x2, yy, 0)
            self.to_core(x2, yy, 0)
            self.arrived(1, 2, j, x2, yy, 1)
            self.to_core(x2, yy, 1)
        for d in self.core:
            d.wait_recv()

    def drain(self):
        for d in self.started:
            d.wait_send()


def ring_sems():
    sem = pltpu.SemaphoreType.DMA
    return [sem((2,)), sem((2,)), sem((2, 3, 2)), sem((2, 3, 2)), sem((16,)), sem((16,))]


def seams(s, x, y, c):
    h = (y + (s % 8) // 7) % 2
    to_left = ((s + 15) % 16, bond(x, (y + ((s + 7) % 8) // 7) % 2, c))
    from_right = ((s + 1) % 16, bond(x, h, c))
    return h, to_left, from_right


def gather_kernel(own, out, zs, zr, *sems):
    s, x, y, c = place()
    h, to_left, from_right = seams(s, x, y, c)
    ring = Ring(out, sems, s, x, y, c, h)
    greet([from_right] + ring.partners, 5)
    z = []
    for k in range(2):
        d = rcopy(
            own.at[pl.ds(128 * k, 128)], out.at[c * 8 + x * 2 + y, pl.ds(128 * k, 128)],
            zs.at[k], zr.at[k], to_left,
        )
        d.start()
        z.append(d)
    for k in range(2):
        z[k].wait_recv()
        ring.home(k)
    ring.rest()
    for d in z:
        d.wait_send()
    ring.drain()


def gather(own, cid):
    sem = pltpu.SemaphoreType.DMA
    return pl.pallas_call(
        gather_kernel,
        name="gather%d" % cid,
        out_shape=jax.ShapeDtypeStruct((16, 256, CHI), BF16),
        in_specs=[ANY],
        out_specs=ANY,
        scratch_shapes=[sem((2,)), sem((2,))] + ring_sems(),
        compiler_params=params(cid),
    )(own)


BLOCKS = [(0, 0), (1, 0), (1, 1), (2, 0), (2, 1), (2, 2), (3, 0), (3, 1), (3, 2), (3, 3)]


def theta_kernel(a, b, proj, gate3, theta, sketch, pay, raw):
    a_val = a[...]

    def raw_step(t, _):
        cols = pl.ds(pl.multiple_of(t * CHI, CHI), CHI)
        rows = pl.ds(pl.multiple_of(t * 32, 32), 32)
        acc = None
        for c in range(2):
            slots = [(i % 2) * 8 + i // 2 for i in range(8 * c, 8 * c + 8)]
            if len(b.shape) == 3:
                part = jnp.concatenate([b[i, rows, :] for i in slots], axis=0)
            else:
                part = jnp.concatenate(
                    [jnp.concatenate([b[k, i, rows, :] for i in slots], axis=0) for k in range(4)],
                    axis=1,
                )
            term = jnp.dot(a_val[:, c * 256:(c + 1) * 256], part, preferred_element_type=F32)
            acc = term if acc is None else acc + term
        raw[:, cols] = acc
        return 0

    lax.fori_loop(0, PHYS, raw_step, 0)
    g3 = gate3[...]

    def gate_step(i, ss):
        halves = []
        for e in range(2):
            rows = pl.ds(pl.multiple_of(i * 16, 16) + 8 * e, 8)
            xr = jnp.concatenate(
                [raw[rows, t * CHI:(t + 1) * CHI] for t in range(PHYS)], axis=0
            )
            hi = xr.astype(BF16)
            lo = (xr - hi.astype(F32)).astype(BF16)
            x3 = jnp.concatenate([hi, lo, hi], axis=0)
            g = jnp.dot(g3, x3, preferred_element_type=F32)
            for v in range(PHYS):
                gv = g[v * 8:(v + 1) * 8, :]
                ss = ss + gv * gv
            halves.append(g)
        rows = pl.ds(pl.multiple_of(i * 16, 16), 16)
        for v in range(PHYS):
            pair = jnp.concatenate([h[v * 8:(v + 1) * 8, :] for h in halves], axis=0)
            theta[rows, v * CHI:(v + 1) * CHI] = pair.astype(BF16)
        return ss

    ss = lax.fori_loop(0, 16, gate_step, jnp.zeros((8, CHI), F32))
    ss = (ss[:, 0:128] + ss[:, 128:256]) + (ss[:, 256:384] + ss[:, 384:512])
    sk = jnp.dot(theta[...], proj[...], preferred_element_type=F32)
    sketch[...] = sk
    skt = sk.T
    for n, (bi, bj) in enumerate(BLOCKS):
        blk = lax.dot_general(
            skt[bi * 128:(bi + 1) * 128, :], sk[:, bj * 128:(bj + 1) * 128],
            (((1,), (0,)), ((), ())), precision=HI, preferred_element_type=F32,
        )
        r = 128 * n
        while r < 128 * n + 128:
            p, o = r // 80, r % 80
            e = min(80 - o, 128 * n + 128 - r)
            pay[p, o:o + e, :] = blk[r - 128 * n:r - 128 * n + e, :]
            r += e
    for p in range(16):
        pay[p, 80:88, :] = ss


def theta_call(a, b, proj, gate3):
    return pl.pallas_call(
        theta_kernel,
        name="theta",
        out_shape=[
            jax.ShapeDtypeStruct((256, PHYS * CHI), BF16),
            jax.ShapeDtypeStruct((256, CHI), F32),
            jax.ShapeDtypeStruct((16, 88, 128), F32),
        ],
        in_specs=[VMEM] * 4,
        out_specs=[VMEM] * 3,
        scratch_shapes=[pltpu.VMEM((256, PHYS * CHI), F32)],
        compiler_params=params(),
    )(a, b, proj, gate3)


def gram_kernel(pay, out, half, rb0, rb1, s0, r0, s1, r1, s2, r2, s3, r3):
    s, x, y, c = place()
    me = x * 2 + y
    c_dev = (s, bond(x, y, 1 - c))
    peers = []
    for k in range(1, 8):
        q = (me + k) % 8
        peers.append((k, q, (s, bond(q // 2, q % 2, c))))
    greet([c_dev] + [p[2] for p in peers], 8)

    first = rcopy(pay.at[pl.ds((1 - c) * 8, 8)], rb0, s0, r0, c_dev)
    first.start()
    first.wait_recv()
    half[...] = pay[pl.ds(c * 8, 8)] + rb0[...]
    sends = [first]
    recvs = []
    for k, q, dev in peers:
        d = rcopy(half.at[q], rb1.at[k - 1], s1.at[k - 1], r1.at[k - 1], dev)
        d.start()
        sends.append(d)
        recvs.append(d)
    acc = half[me]
    for d in recvs:
        d.wait_recv()
    t = [rb1[k] for k in range(7)]
    mine = ((acc + t[0]) + (t[1] + t[2])) + ((t[3] + t[4]) + (t[5] + t[6]))
    slot = c * 8 + me
    out[slot] = mine
    bcast = []
    for k, q, dev in peers:
        d = rcopy(out.at[slot], out.at[slot], s2.at[k - 1], r2.at[k - 1], dev)
        d.start()
        sends.append(d)
        bcast.append(d)
    core = []
    d = rcopy(out.at[slot], out.at[slot], s3.at[0], r3.at[0], c_dev)
    d.start()
    core.append(d)
    for k in range(1, 8):
        bcast[k - 1].wait_recv()
        src = c * 8 + (me + 8 - k) % 8
        d = rcopy(out.at[src], out.at[src], s3.at[k], r3.at[k], c_dev)
        d.start()
        core.append(d)
    for d in core:
        d.wait_recv()
    for d in sends + core:
        d.wait_send()


def gram_call(pay, cid):
    sem = pltpu.SemaphoreType.DMA
    return pl.pallas_call(
        gram_kernel,
        name="gram%d" % cid,
        out_shape=jax.ShapeDtypeStruct((16, 88, 128), F32),
        in_specs=[VMEM],
        out_specs=VMEM,
        scratch_shapes=[
            pltpu.VMEM((8, 88, 128), F32), pltpu.VMEM((8, 88, 128), F32),
            pltpu.VMEM((7, 88, 128), F32),
            sem, sem, sem((7,)), sem((7,)), sem((7,)), sem((7,)), sem((8,)), sem((8,)),
        ],
        compiler_params=params(cid),
    )(pay)


def bl(v, k):
    return jnp.broadcast_to(v[:, k:k + 1], (8, 128))


def bs(v, j):
    return jnp.broadcast_to(v[j:j + 1, :], (8, 128))


def leaf(rows, hook):
    lane = lax.broadcasted_iota(jnp.int32, (8, 128), 1)
    sub = lax.broadcasted_iota(jnp.int32, (8, 128), 0)
    rows = list(rows)
    out = []
    n = len(rows)
    for p in range(n):
        m_p = rows[p]
        c = [bl(m_p, 8 * p + v) for v in range(8)]
        pc = (lane >= 8 * p) & (lane < 8 * p + 8)
        m_p = jnp.where(pc, jnp.where(lane - 8 * p == sub, 1.0, 0.0), m_p)
        fwd = m_p
        diag = None
        for j in range(8):
            d = bs(c[j], j)
            isj = sub == j
            mult = jnp.where(isj, 0.0, c[j] * (1.0 / d))
            if j:
                diag = jnp.where(isj, d, diag)
                fwd = jnp.where(isj, m_p, fwd)
            else:
                diag = d
            for v in range(j + 1, 8):
                c[v] = c[v] - mult * bs(c[v], j)
            m_p = m_p - mult * bs(m_p, j)
        out.append(jnp.where(lane < 8 * p + 8, fwd * lax.rsqrt(diag), 0.0))
        if p == n - 1:
            break
        yy = m_p * (1.0 / diag)
        yb = [bs(yy, v) for v in range(8)]
        for q in range(p + 1, n):
            t = [bl(rows[q], 8 * p + v) * yb[v] for v in range(8)]
            tot = ((t[0] + t[1]) + (t[2] + t[3])) + ((t[4] + t[5]) + (t[6] + t[7]))
            rows[q] = jnp.where(pc, 0.0, rows[q]) - tot
        hook(p)
    return out


def dott(a, b):
    return lax.dot_general(
        a, b, (((1,), (1,)), ((), ())), precision=HI, preferred_element_type=F32
    )


def dotn(a, b):
    return lax.dot_general(
        a, b, (((1,), (0,)), ((), ())), precision=HI, preferred_element_type=F32
    )


def unpack_gram(pay, a):
    for n, (bi, bj) in enumerate(BLOCKS):
        r = 128 * n
        while r < 128 * n + 128:
            p, o = r // 80, r % 80
            e = min(80 - o, 128 * n + 128 - r)
            q = bi * 128 + r - 128 * n
            a[q:q + e, bj * 128:(bj + 1) * 128] = pay[p, o:o + e, :]
            r += e


def mid_kernel(parity, *refs):
    first = parity == 0
    refs = list(refs)
    pay, sketch, theta, left, rcol, log = refs[:6]
    refs = refs[6:]
    if first:
        bout, lp, zs, zr, gxs, gxr, gcs, gcr = refs[:1] + refs[-7:]
        refs = refs[1:-7]
    a, linv, part, rbc, rbd, fin = refs[:6]
    cs, cr, ds, dr, as_, ar = refs[6:]

    s, x, y, c = place()
    is_left = s % 2 == parity
    _, to_left, from_right = seams(s, x, y, c)
    c_dev = (s, bond(x, y, 1 - c))
    right, before = (s + 1) % 16, (s + 15) % 16
    others = [(x * 2 + y + k) % 8 for k in range(1, 8)]
    greet(
        [c_dev] + [(s, bond(q // 2, q % 2, c)) for q in others]
        + [(before, q) for q in range(16)] + ([from_right] if first else []),
        25 if first else 24,
    )
    me = c * 8 + x * 2 + y
    root = math.sqrt(PHYS * CHI)

    @pl.when(is_left)
    def _():
        sent = []

        def send(src, dst, ss, rs, dev):
            d = rcopy(src, dst, ss, rs, dev)
            d.start()
            sent.append(d)
            return d

        total = jnp.sum(jnp.sum(pay[0, 80:88, :], axis=0, keepdims=True), axis=1, keepdims=True)
        mean_square = total * (1.0 / (CHI * PHYS * PHYS * CHI)) + epsilon
        log[...] = jnp.broadcast_to(0.5 * jnp.log(mean_square), (8, 128))
        scale = lax.rsqrt(mean_square) * (1.0 / root)
        unpack_gram(pay, a)
        ri = lax.broadcasted_iota(jnp.int32, (256, 256), 0)
        ci = lax.broadcasted_iota(jnp.int32, (256, 256), 1)
        perm = jnp.where(ci == (ri % 32) * 8 + ri // 32, 1.0, 0.0).astype(BF16)
        core, peers = {}, {}

        def publish(b):
            o = b * 128
            ln = (dott(sketch[:, :o + 128], linv[o:o + 128, :o + 128]) * root).astype(BF16)
            left[:, o:o + 128] = ln
            if first:
                lp[b] = jnp.dot(perm, ln, preferred_element_type=F32).astype(BF16)
                send(lp.at[b], bout.at[b, me], zs.at[b], zr.at[b], to_left)
            lnt = ln.astype(F32).T.astype(BF16)
            for t in range(PHYS):
                blk = jnp.dot(
                    lnt, theta[:, t * CHI:(t + 1) * CHI], preferred_element_type=F32
                )
                blk = (blk * scale).astype(BF16)
                part[b, 2 * t] = blk[:, 0:256]
                part[b, 2 * t + 1] = blk[:, 256:512]
            core[b] = send(
                part.at[b, pl.ds((1 - c) * 8, 8)], rbc.at[b], cs.at[b], cr.at[b], c_dev
            )

        def step_a(b):
            core[b].wait_recv()
            half = part[b, pl.ds(c * 8, 8)].astype(F32) + rbc[b].astype(F32)
            part[b, pl.ds(c * 8, 8)] = half.astype(BF16)
            peers[b] = [
                send(
                    part.at[b, c * 8 + q], rbd.at[b, k], ds.at[b, k], dr.at[b, k],
                    (s, bond(q // 2, q % 2, c)),
                )
                for k, q in enumerate(others)
            ]

        def step_d(b):
            for d in peers[b]:
                d.wait_recv()
            t = [rbd[b, k].astype(F32) for k in range(7)]
            tot = ((part[b, me].astype(F32) + t[0]) + (t[1] + t[2])) + (
                (t[3] + t[4]) + (t[5] + t[6]))
            fin[b] = tot.astype(BF16)
            for i in range(4):
                send(
                    fin.at[b, pl.ds(32 * i, 32)], rcol.at[me], as_.at[b, i], ar.at[me],
                    (right, 4 * b + i),
                )

        plan = {
            1: {9: [(step_a, 0)]},
            2: {9: [(step_a, 1)], 13: [(step_d, 0)]},
            3: {9: [(step_a, 2)], 13: [(step_d, 1)]},
        }
        for b in range(4):
            o = b * 128
            t = dotn(a[o:o + 128, :o], linv[:o, :o]) if b else None

            def hook(p, b=b):
                for f, arg in plan.get(b, {}).get(p, ()):
                    f(arg)

            inv = jnp.concatenate(
                leaf([a[o + 8 * q:o + 8 * q + 8, o:o + 128] for q in range(16)], hook), 0
            )
            linv[o:o + 128, o:o + 128] = inv
            if b < 3:
                linv[o:o + 128, o + 128:] = jnp.zeros((128, CHI - o - 128), F32)
            if b > 0:
                linv[o:o + 128, :o] = -dotn(inv, t)
            publish(b)
            if b < 3:
                lb = dott(a[o + 128:, o:o + 128], inv)
                a[o + 128:, o:o + 128] = lb
                a[o + 128:, o + 128:] = a[o + 128:, o + 128:] - dott(lb, lb)
        step_a(3)
        step_d(2)
        step_d(3)
        for d in sent:
            d.wait_send()

    @pl.when(jnp.logical_not(is_left))
    def _():
        if first:
            seam = (s % 8) // 7
            sent, cores = [], []

            def slot(b, q):
                return bout.at[b, c * 8 + (q // 2) * 2 + (q % 2 + seam) % 2]

            def send(ref, ss, rs, dev):
                d = rcopy(ref, ref, ss, rs, dev)
                d.start()
                sent.append(d)
                return d

            def here(ref, rs):
                pltpu.make_async_copy(ref, ref, rs).wait()

            mine = x * 2 + y
            for b in range(5):
                if b < 4:
                    ref = slot(b, mine)
                    here(ref, zr.at[b])
                    for k, q in enumerate(others):
                        send(ref, gxs.at[b, k], gxr.at[b, k], (s, bond(q // 2, q % 2, c)))
                    cores.append(send(ref, gcs.at[b, 7], gcr.at[b, 7], c_dev))
                if b > 0:
                    for k in range(7):
                        ref = slot(b - 1, (mine + 7 - k) % 8)
                        here(ref, gxr.at[b - 1, k])
                        cores.append(send(ref, gcs.at[b - 1, k], gcr.at[b - 1, k], c_dev))
            for d in cores:
                d.wait_recv()
            for d in sent:
                d.wait_send()
        for q in range(16):
            pltpu.make_async_copy(rcol.at[q], rcol.at[q], ar.at[q]).wait()


def mid_call(pay, sketch, theta, parity, cid):
    sem = pltpu.SemaphoreType.DMA
    first = parity == 0
    outs = [
        jax.ShapeDtypeStruct((256, CHI), BF16),
        jax.ShapeDtypeStruct((16, 32, 256), BF16),
        jax.ShapeDtypeStruct((8, 128), F32),
    ]
    scratch = [
        pltpu.VMEM((CHI, CHI), F32), pltpu.VMEM((CHI, CHI), F32),
        pltpu.VMEM((4, 16, 128, 256), BF16), pltpu.VMEM((4, 8, 128, 256), BF16),
        pltpu.VMEM((4, 7, 128, 256), BF16), pltpu.VMEM((4, 128, 256), BF16),
        sem((4,)), sem((4,)), sem((4, 7)), sem((4, 7)), sem((4, 4)), sem((16,)),
    ]
    if first:
        outs.append(jax.ShapeDtypeStruct((4, 16, 256, 128), BF16))
        scratch += [
            pltpu.VMEM((4, 256, 128), BF16), sem((4,)), sem((4,)),
            sem((4, 7)), sem((4, 7)), sem((4, 8)), sem((4, 8)),
        ]
    return pl.pallas_call(
        functools.partial(mid_kernel, parity),
        name="mid%d" % cid,
        out_shape=outs,
        in_specs=[VMEM] * 3,
        out_specs=[VMEM] * len(outs),
        scratch_shapes=scratch,
        compiler_params=params(cid),
    )(pay, sketch, theta)


def gate_split(gates, position):
    g = lax.dynamic_index_in_dim(gates, position, 0, keepdims=False)
    g = g.reshape(8, 8, 8, 8).transpose(1, 0, 3, 2).reshape(64, 64)
    hi = lax.reduce_precision(g, 8, 7)
    lo = (g - hi).astype(BF16)
    hi = hi.astype(BF16)
    return jnp.concatenate([hi, hi, lo], axis=1)


def shards(mps, projection, gates):
    position = lax.axis_index("site")
    gate3 = gate_split(gates, position)
    proj = projection[0]
    b = gather(mps[0].transpose(1, 0, 2).reshape(256, CHI), 0)
    a = mps[0].reshape(256, CHI)
    logs, tensors = [], []
    for parity in range(2):
        theta, sketch, pay = theta_call(a, b, proj, gate3)
        pay = gram_call(pay, 3 * parity + 1)
        left, rcol, log, *more = mid_call(pay, sketch, theta, parity, 3 * parity + 2)
        b = more[0] if more else None
        a = rcol.reshape(PHYS, 2, 32, 256).transpose(2, 0, 1, 3).reshape(256, CHI)
        logs.append(log[0, 0:1])
        tensors.append(left)
    odd = position % 2 == 1
    state = jnp.where(odd, tensors[1], a).reshape(32, PHYS, CHI)
    return state[None], jnp.where(odd, logs[1], logs[0])


def solution(mesh):
    return jax.shard_map(
        shards,
        mesh=mesh,
        in_specs=(P("site", "bond", None, None), P("site", None, None), P()),
        out_specs=(P("site", "bond", None, None), P("site")),
        check_vma=False,
    )
```

```python
import functools
import math

import jax
import jax.numpy as jnp
from jax import lax
from jax.experimental import pallas as pl
from jax.experimental.pallas import tpu as pltpu
from jax.sharding import PartitionSpec as P

PHYS = 8
CHI = 512
epsilon = 1e-06
MESH = pl.DeviceIdType.MESH
HI = lax.Precision.HIGHEST
F32 = jnp.float32
BF16 = jnp.bfloat16
VMEM = pl.BlockSpec(memory_space=pltpu.VMEM)
ANY = pl.BlockSpec(memory_space=pl.ANY)
VLIM = 56 << 20


def params(cid=None):
    if cid is None:
        return pltpu.CompilerParams(vmem_limit_bytes=VLIM)
    return pltpu.CompilerParams(
        collective_id=cid, has_side_effects=True, vmem_limit_bytes=VLIM
    )


def place():
    s = lax.axis_index("site")
    b = lax.axis_index("bond")
    return s, b // 4, (b // 2) % 2, b % 2


def bond(x, y, c):
    return (x * 2 + y) * 2 + c


def greet(sends_to_me, count):
    barrier = pltpu.get_barrier_semaphore()
    for dev in sends_to_me:
        pl.semaphore_signal(barrier, inc=1, device_id=dev, device_id_type=MESH)
    pl.semaphore_wait(barrier, count)


def swap_rows(value, inner):
    n = value.shape[0]
    ri = lax.broadcasted_iota(jnp.int32, (n, n), 0)
    ci = lax.broadcasted_iota(jnp.int32, (n, n), 1)
    outer = n // inner
    perm = jnp.where(ci == (ri % outer) * inner + ri // outer, 1.0, 0.0).astype(BF16)
    return jnp.dot(perm, value, preferred_element_type=F32).astype(BF16)


def rcopy(src, dst, ssem, rsem, dev):
    return pltpu.make_async_remote_copy(
        src_ref=src, dst_ref=dst, send_sem=ssem, recv_sem=rsem,
        device_id=dev, device_id_type=MESH,
    )


class Ring:
    def __init__(self, out, sems, s, x, y, c, h):
        self.out, self.c = out, c
        self.ys, self.yr, self.xs, self.xr, self.cs, self.cr = sems
        self.x, self.h = x, h
        self.xp, self.xm, self.x2 = (x + 1) % 4, (x + 3) % 4, (x + 2) % 4
        self.hn = 1 - h
        self.y_dev = (s, bond(x, 1 - y, c))
        self.xp_dev = (s, bond(self.xp, y, c))
        self.xm_dev = (s, bond(self.xm, y, c))
        self.c_dev = (s, bond(x, y, 1 - c))
        self.partners = [self.y_dev, self.xp_dev, self.xm_dev, self.c_dev]
        self.started, self.core, self.ysend = [], [], []

    def slot(self, xx, yy, k):
        return self.out.at[self.c * 8 + xx * 2 + yy, pl.ds(128 * k, 128)]

    def send(self, ref, ss, rs, dev):
        d = rcopy(ref, ref, ss, rs, dev)
        d.start()
        self.started.append(d)
        return d

    def to_core(self, xx, yy, k):
        i = len(self.core)
        ref = self.slot(xx, yy, k)
        self.core.append(self.send(ref, self.cs.at[i], self.cr.at[i], self.c_dev))

    def home(self, k):
        ref = self.slot(self.x, self.h, k)
        self.ysend.append(self.send(ref, self.ys.at[k], self.yr.at[k], self.y_dev))
        for i, dev in enumerate((self.xp_dev, self.xm_dev)):
            self.send(ref, self.xs.at[i, 0, k], self.xr.at[i, 0, k], dev)
        self.to_core(self.x, self.h, k)

    def arrived(self, i, j, k, xx, yy, part):
        ref = self.slot(xx, yy, part)
        pltpu.make_async_copy(ref, ref, self.xr.at[i, j, k]).wait()

    def rest(self):
        x, h, hn, xp, xm, x2 = self.x, self.h, self.hn, self.xp, self.xm, self.x2
        xs, xr = self.xs, self.xr
        for k in range(2):
            self.ysend[k].wait_recv()
            for i, dev in enumerate((self.xp_dev, self.xm_dev)):
                self.send(self.slot(x, hn, k), xs.at[i, 1, k], xr.at[i, 1, k], dev)
            self.to_core(x, hn, k)
        for j, yy in ((0, h), (1, hn)):
            for k in range(2):
                self.arrived(0, j, k, xm, yy, k)
                if k == 0:
                    self.send(self.slot(xm, yy, 0), xs.at[0, 2, j], xr.at[0, 2, j], self.xp_dev)
                self.to_core(xm, yy, k)
                self.arrived(1, j, k, xp, yy, k)
                if k == 1:
                    self.send(self.slot(xp, yy, 1), xs.at[1, 2, j], xr.at[1, 2, j], self.xm_dev)
                self.to_core(xp, yy, k)
        for j, yy in ((0, h), (1, hn)):
            self.arrived(0, 2, j, x2, yy, 0)
            self.to_core(x2, yy, 0)
            self.arrived(1, 2, j, x2, yy, 1)
            self.to_core(x2, yy, 1)
        for d in self.core:
            d.wait_recv()

    def drain(self):
        for d in self.started:
            d.wait_send()


def ring_sems():
    sem = pltpu.SemaphoreType.DMA
    return [sem((2,)), sem((2,)), sem((2, 3, 2)), sem((2, 3, 2)), sem((16,)), sem((16,))]


def seams(s, x, y, c):
    h = (y + (s % 8) // 7) % 2
    to_left = ((s + 15) % 16, bond(x, (y + ((s + 7) % 8) // 7) % 2, c))
    from_right = ((s + 1) % 16, bond(x, h, c))
    return h, to_left, from_right


def gather_kernel(mine, out, own, zs, zr, *sems):
    s, x, y, c = place()
    h, to_left, from_right = seams(s, x, y, c)
    ring = Ring(out, sems, s, x, y, c, h)
    own[...] = swap_rows(mine[...], PHYS)
    greet([from_right] + ring.partners, 5)
    z = []
    for k in range(2):
        d = rcopy(
            own.at[pl.ds(128 * k, 128)], out.at[c * 8 + x * 2 + y, pl.ds(128 * k, 128)],
            zs.at[k], zr.at[k], to_left,
        )
        d.start()
        z.append(d)
    for k in range(2):
        z[k].wait_recv()
        ring.home(k)
    ring.rest()
    for d in z:
        d.wait_send()
    ring.drain()


def gather(own, cid):
    sem = pltpu.SemaphoreType.DMA
    return pl.pallas_call(
        gather_kernel,
        name="gather%d" % cid,
        out_shape=jax.ShapeDtypeStruct((16, 256, CHI), BF16),
        in_specs=[VMEM],
        out_specs=ANY,
        scratch_shapes=[pltpu.VMEM((256, CHI), BF16), sem((2,)), sem((2,))] + ring_sems(),
        compiler_params=params(cid),
    )(own)


BLOCKS = [(0, 0), (1, 0), (1, 1), (2, 0), (2, 1), (2, 2), (3, 0), (3, 1), (3, 2), (3, 3)]


def theta_kernel(a, b, proj, gates, theta, sketch, pay_a, pay_b, raw):
    a_val = a[...]

    def raw_step(t, _):
        cols = pl.ds(pl.multiple_of(t * CHI, CHI), CHI)
        rows = pl.ds(pl.multiple_of(t * 32, 32), 32)
        acc = None
        for c in range(2):
            slots = [(i % 2) * 8 + i // 2 for i in range(8 * c, 8 * c + 8)]
            if len(b.shape) == 3:
                part = jnp.concatenate([b[i, rows, :] for i in slots], axis=0)
            else:
                part = jnp.concatenate(
                    [jnp.concatenate([b[k, i, rows, :] for i in slots], axis=0) for k in range(4)],
                    axis=1,
                )
            term = jnp.dot(a_val[:, c * 256:(c + 1) * 256], part, preferred_element_type=F32)
            acc = term if acc is None else acc + term
        raw[:, cols] = acc
        return 0

    lax.fori_loop(0, PHYS, raw_step, 0)
    gate = gates[lax.axis_index("site")]
    g_hi = gate.astype(BF16)
    g_lo = (gate - g_hi.astype(F32)).astype(BF16)
    g_hi, g_lo = [
        swap_rows(swap_rows(g, 8).astype(F32).T.astype(BF16), 8).astype(F32).T.astype(BF16)
        for g in (g_hi, g_lo)
    ]
    g3 = jnp.concatenate([g_hi, g_hi, g_lo], axis=1)

    def gate_step(i, ss):
        halves = []
        for e in range(2):
            rows = pl.ds(pl.multiple_of(i * 16, 16) + 8 * e, 8)
            xr = jnp.concatenate(
                [raw[rows, t * CHI:(t + 1) * CHI] for t in range(PHYS)], axis=0
            )
            hi = xr.astype(BF16)
            lo = (xr - hi.astype(F32)).astype(BF16)
            x3 = jnp.concatenate([hi, lo, hi], axis=0)
            g = jnp.dot(g3, x3, preferred_element_type=F32)
            for v in range(PHYS):
                gv = g[v * 8:(v + 1) * 8, :]
                ss = ss + gv * gv
            halves.append(g)
        rows = pl.ds(pl.multiple_of(i * 16, 16), 16)
        for v in range(PHYS):
            pair = jnp.concatenate([h[v * 8:(v + 1) * 8, :] for h in halves], axis=0)
            theta[rows, v * CHI:(v + 1) * CHI] = pair.astype(BF16)
        return ss

    ss = lax.fori_loop(0, 16, gate_step, jnp.zeros((8, CHI), F32))
    ss = (ss[:, 0:128] + ss[:, 128:256]) + (ss[:, 256:384] + ss[:, 384:512])
    sk = jnp.dot(theta[...], proj[...], preferred_element_type=F32)
    sketch[...] = sk
    skt = sk.T
    for n, (bi, bj) in enumerate(BLOCKS):
        blk = lax.dot_general(
            skt[bi * 128:(bi + 1) * 128, :], sk[:, bj * 128:(bj + 1) * 128],
            (((1,), (0,)), ((), ())), precision=HI, preferred_element_type=F32,
        )
        if n == 0:
            for p in range(16):
                pay_a[p, 0:8, :] = blk[8 * p:8 * p + 8, :]
            continue
        r = 128 * (n - 1)
        while r < 128 * n:
            p, o = r // 72, r % 72
            e = min(72 - o, 128 * n - r)
            pay_b[p, o:o + e, :] = blk[r - 128 * (n - 1):r - 128 * (n - 1) + e, :]
            r += e
    for p in range(16):
        pay_a[p, 8:16, :] = ss


def theta_call(a, b, proj, gates):
    return pl.pallas_call(
        theta_kernel,
        name="theta",
        out_shape=[
            jax.ShapeDtypeStruct((256, PHYS * CHI), BF16),
            jax.ShapeDtypeStruct((256, CHI), F32),
            jax.ShapeDtypeStruct((16, 16, 128), F32),
            jax.ShapeDtypeStruct((16, 72, 128), F32),
        ],
        in_specs=[VMEM] * 4,
        out_specs=[VMEM] * 4,
        scratch_shapes=[pltpu.VMEM((256, PHYS * CHI), F32)],
        compiler_params=params(),
    )(a, b, proj, gates)


class Sum:
    def __init__(self, pay, half, rb0, rb1, out, sems, c, me, c_dev, devs, sent):
        self.pay, self.half, self.rb0, self.rb1, self.out = pay, half, rb0, rb1, out
        self.sems, self.c, self.me, self.c_dev, self.devs = sems, c, me, c_dev, devs
        self.sent, self.cores = sent, []

    def send(self, src, dst, i, k, dev):
        d = rcopy(src, dst, self.sems[2 * i].at[k], self.sems[2 * i + 1].at[k], dev)
        d.start()
        self.sent.append(d)
        return d

    def begin(self):
        self.core = self.send(self.pay.at[pl.ds((1 - self.c) * 8, 8)], self.rb0, 0, 0, self.c_dev)

    def scatter(self):
        self.core.wait_recv()
        self.half[...] = self.pay[pl.ds(self.c * 8, 8)] + self.rb0[...]
        self.parts = [
            self.send(self.half.at[(self.me + k + 1) % 8], self.rb1.at[k], 1, k, dev)
            for k, dev in enumerate(self.devs)
        ]

    def spread(self):
        for d in self.parts:
            d.wait_recv()
        t = [self.rb1[k] for k in range(7)]
        slot = self.c * 8 + self.me
        self.out[slot] = ((self.half[self.me] + t[0]) + (t[1] + t[2])) + (
            (t[3] + t[4]) + (t[5] + t[6]))
        ref = self.out.at[slot]
        self.wide = [self.send(ref, ref, 2, k, dev) for k, dev in enumerate(self.devs)]
        self.cores.append(self.send(ref, ref, 3, 7, self.c_dev))

    def forward(self):
        for k in range(7):
            self.wide[k].wait_recv()
            ref = self.out.at[self.c * 8 + (self.me + 7 - k) % 8]
            self.cores.append(self.send(ref, ref, 3, k, self.c_dev))

    def finish(self):
        for d in self.cores:
            d.wait_recv()


def sum_scratch(rows):
    sem = pltpu.SemaphoreType.DMA
    return [
        pltpu.VMEM((8, rows, 128), F32), pltpu.VMEM((8, rows, 128), F32),
        pltpu.VMEM((7, rows, 128), F32), pltpu.VMEM((16, rows, 128), F32),
        sem((1,)), sem((1,)), sem((7,)), sem((7,)), sem((7,)), sem((7,)), sem((8,)), sem((8,)),
    ]


def bl(v, k):
    return jnp.broadcast_to(v[:, k:k + 1], (8, 128))


def bs(v, j):
    return jnp.broadcast_to(v[j:j + 1, :], (8, 128))


def leaf(rows, hook):
    lane = lax.broadcasted_iota(jnp.int32, (8, 128), 1)
    sub = lax.broadcasted_iota(jnp.int32, (8, 128), 0)
    rows = list(rows)
    out = []
    n = len(rows)
    for p in range(n):
        m_p = rows[p]
        c = [bl(m_p, 8 * p + v) for v in range(8)]
        pc = (lane >= 8 * p) & (lane < 8 * p + 8)
        m_p = jnp.where(pc, jnp.where(lane - 8 * p == sub, 1.0, 0.0), m_p)
        fwd = m_p
        diag = None
        for j in range(8):
            d = bs(c[j], j)
            isj = sub == j
            mult = jnp.where(isj, 0.0, c[j] * (1.0 / d))
            if j:
                diag = jnp.where(isj, d, diag)
                fwd = jnp.where(isj, m_p, fwd)
            else:
                diag = d
            for v in range(j + 1, 8):
                c[v] = c[v] - mult * bs(c[v], j)
            m_p = m_p - mult * bs(m_p, j)
        out.append(jnp.where(lane < 8 * p + 8, fwd * lax.rsqrt(diag), 0.0))
        if p == n - 1:
            break
        yy = m_p * (1.0 / diag)
        yb = [bs(yy, v) for v in range(8)]
        for q in range(p + 1, n):
            t = [bl(rows[q], 8 * p + v) * yb[v] for v in range(8)]
            tot = ((t[0] + t[1]) + (t[2] + t[3])) + ((t[4] + t[5]) + (t[6] + t[7]))
            rows[q] = jnp.where(pc, 0.0, rows[q]) - tot
        hook(p)
    return out


def dott(a, b):
    return lax.dot_general(
        a, b, (((1,), (1,)), ((), ())), precision=HI, preferred_element_type=F32
    )


def dotn(a, b):
    return lax.dot_general(
        a, b, (((1,), (0,)), ((), ())), precision=HI, preferred_element_type=F32
    )


def unpack_rest(pay, a):
    for n, (bi, bj) in enumerate(BLOCKS[1:]):
        r = 128 * n
        while r < 128 * n + 128:
            p, o = r // 72, r % 72
            e = min(72 - o, 128 * n + 128 - r)
            q = bi * 128 + r - 128 * n
            a[q:q + e, bj * 128:(bj + 1) * 128] = pay[p, o:o + e, :]
            r += e


def mid_kernel(parity, *refs):
    first = parity == 0
    refs = list(refs)
    pay_a, pay_b, sketch, theta, left, log = refs[:6]
    refs = refs[6:]
    if first:
        bout, lp, zs, zr, gxs, gxr, gcs, gcr = refs[:1] + refs[-7:]
        refs = refs[1:-7]
    a, linv, part, rbc, rbd, fin, rcol = refs[:7]
    cs, cr, ds, dr, as_, ar = refs[7:13]
    scr_a, scr_b = refs[13:25], refs[25:37]

    s, x, y, c = place()
    is_left = s % 2 == parity
    _, to_left, from_right = seams(s, x, y, c)
    c_dev = (s, bond(x, y, 1 - c))
    right, before = (s + 1) % 16, (s + 15) % 16
    others = [(x * 2 + y + k) % 8 for k in range(1, 8)]
    greet(
        [c_dev] + [(s, bond(q // 2, q % 2, c)) for q in others]
        + [(before, q) for q in range(16)] + ([from_right] if first else []),
        25 if first else 24,
    )
    me = c * 8 + x * 2 + y
    root = math.sqrt(PHYS * CHI)

    @pl.when(is_left)
    def _():
        sent = []

        def send(src, dst, ss, rs, dev):
            d = rcopy(src, dst, ss, rs, dev)
            d.start()
            sent.append(d)
            return d

        devs = [(s, bond(q // 2, q % 2, c)) for q in others]
        sums = [
            Sum(pay, *scr[:4], scr[4:], c, x * 2 + y, c_dev, devs, sent)
            for pay, scr in ((pay_a, scr_a), (pay_b, scr_b))
        ]
        for f in ("begin", "scatter", "spread"):
            for v in sums:
                getattr(v, f)()
        sums[0].forward()
        sums[0].finish()
        gram = scr_a[3]
        total = jnp.sum(jnp.sum(gram[0, 8:16, :], axis=0, keepdims=True), axis=1, keepdims=True)
        mean_square = total * (1.0 / (CHI * PHYS * PHYS * CHI)) + epsilon
        log[...] = jnp.broadcast_to(0.5 * jnp.log(mean_square), (8, 128))
        scale = lax.rsqrt(mean_square) * (1.0 / root)
        for p in range(16):
            a[8 * p:8 * p + 8, 0:128] = gram[p, 0:8, :]
        core, peers = {}, {}

        def publish(b):
            o = b * 128
            ln = (dott(sketch[:, :o + 128], linv[o:o + 128, :o + 128]) * root).astype(BF16)
            left[:, o:o + 128] = ln
            if first:
                lp[b] = swap_rows(ln, PHYS)
                send(lp.at[b], bout.at[b, me], zs.at[b], zr.at[b], to_left)
            lnt = ln.astype(F32).T.astype(BF16)
            for t in range(PHYS):
                blk = jnp.dot(
                    lnt, theta[:, t * CHI:(t + 1) * CHI], preferred_element_type=F32
                )
                blk = (blk * scale).astype(BF16)
                part[b, 2 * t] = blk[:, 0:256]
                part[b, 2 * t + 1] = blk[:, 256:512]
            core[b] = send(
                part.at[b, pl.ds((1 - c) * 8, 8)], rbc.at[b], cs.at[b], cr.at[b], c_dev
            )

        def step_a(b):
            core[b].wait_recv()
            half = part[b, pl.ds(c * 8, 8)].astype(F32) + rbc[b].astype(F32)
            part[b, pl.ds(c * 8, 8)] = half.astype(BF16)
            peers[b] = [
                send(
                    part.at[b, c * 8 + q], rbd.at[b, k], ds.at[b, k], dr.at[b, k],
                    (s, bond(q // 2, q % 2, c)),
                )
                for k, q in enumerate(others)
            ]

        def step_d(b):
            for d in peers[b]:
                d.wait_recv()
            t = [rbd[b, k].astype(F32) for k in range(7)]
            tot = ((part[b, me].astype(F32) + t[0]) + (t[1] + t[2])) + (
                (t[3] + t[4]) + (t[5] + t[6]))
            fin[b] = tot.astype(BF16)
            for i in range(4):
                send(
                    fin.at[b, pl.ds(32 * i, 32)], rcol.at[me], as_.at[b, i], ar.at[me],
                    (right, 4 * b + i),
                )

        plan = {
            0: {8: [(lambda _: sums[1].forward(), 0)]},
            1: {9: [(step_a, 0)]},
            2: {9: [(step_a, 1)], 13: [(step_d, 0)]},
            3: {9: [(step_a, 2)], 13: [(step_d, 1)]},
        }
        for b in range(4):
            o = b * 128
            t = dotn(a[o:o + 128, :o], linv[:o, :o]) if b else None

            def hook(p, b=b):
                for f, arg in plan.get(b, {}).get(p, ()):
                    f(arg)

            inv = jnp.concatenate(
                leaf([a[o + 8 * q:o + 8 * q + 8, o:o + 128] for q in range(16)], hook), 0
            )
            linv[o:o + 128, o:o + 128] = inv
            if b < 3:
                linv[o:o + 128, o + 128:] = jnp.zeros((128, CHI - o - 128), F32)
            if b > 0:
                linv[o:o + 128, :o] = -dotn(inv, t)
            publish(b)
            if b == 0:
                sums[1].finish()
                unpack_rest(scr_b[3], a)
            if b < 3:
                lb = dott(a[o + 128:, o:o + 128], inv)
                a[o + 128:, o:o + 128] = lb
                a[o + 128:, o + 128:] = a[o + 128:, o + 128:] - dott(lb, lb)
        step_a(3)
        step_d(2)
        step_d(3)
        for d in sent:
            d.wait_send()

    @pl.when(jnp.logical_not(is_left))
    def _():
        if first:
            seam = (s % 8) // 7
            sent, cores = [], []

            def slot(b, q):
                return bout.at[b, c * 8 + (q // 2) * 2 + (q % 2 + seam) % 2]

            def send(ref, ss, rs, dev):
                d = rcopy(ref, ref, ss, rs, dev)
                d.start()
                sent.append(d)
                return d

            def here(ref, rs):
                pltpu.make_async_copy(ref, ref, rs).wait()

            mine = x * 2 + y
            for b in range(5):
                if b < 4:
                    ref = slot(b, mine)
                    here(ref, zr.at[b])
                    for k, q in enumerate(others):
                        send(ref, gxs.at[b, k], gxr.at[b, k], (s, bond(q // 2, q % 2, c)))
                    cores.append(send(ref, gcs.at[b, 7], gcr.at[b, 7], c_dev))
                if b > 0:
                    for k in range(7):
                        ref = slot(b - 1, (mine + 7 - k) % 8)
                        here(ref, gxr.at[b - 1, k])
                        cores.append(send(ref, gcs.at[b - 1, k], gcr.at[b - 1, k], c_dev))
            for d in cores:
                d.wait_recv()
            for d in sent:
                d.wait_send()
        for q in range(16):
            pltpu.make_async_copy(rcol.at[q], rcol.at[q], ar.at[q]).wait()
        rows = jnp.concatenate(
            [jnp.concatenate([rcol[2 * t], rcol[2 * t + 1]], axis=1) for t in range(PHYS)], axis=0
        )
        left[...] = swap_rows(rows, 32)


def mid_call(pay_a, pay_b, sketch, theta, parity, cid):
    sem = pltpu.SemaphoreType.DMA
    first = parity == 0
    outs = [
        jax.ShapeDtypeStruct((256, CHI), BF16),
        jax.ShapeDtypeStruct((8, 128), F32),
    ]
    scratch = [
        pltpu.VMEM((CHI, CHI), F32), pltpu.VMEM((CHI, CHI), F32),
        pltpu.VMEM((4, 16, 128, 256), BF16), pltpu.VMEM((4, 8, 128, 256), BF16),
        pltpu.VMEM((4, 7, 128, 256), BF16), pltpu.VMEM((4, 128, 256), BF16),
        pltpu.VMEM((16, 32, 256), BF16),
        sem((4,)), sem((4,)), sem((4, 7)), sem((4, 7)), sem((4, 4)), sem((16,)),
    ] + sum_scratch(16) + sum_scratch(72)
    if first:
        outs.append(jax.ShapeDtypeStruct((4, 16, 256, 128), BF16))
        scratch += [
            pltpu.VMEM((4, 256, 128), BF16), sem((4,)), sem((4,)),
            sem((4, 7)), sem((4, 7)), sem((4, 8)), sem((4, 8)),
        ]
    return pl.pallas_call(
        functools.partial(mid_kernel, parity),
        name="mid%d" % cid,
        out_shape=outs,
        in_specs=[VMEM] * 4,
        out_specs=[VMEM] * len(outs),
        scratch_shapes=scratch,
        compiler_params=params(cid),
    )(pay_a, pay_b, sketch, theta)


def shards(mps, projection, gates):
    proj = projection[0]
    a = mps[0].reshape(256, CHI)
    b = gather(a, 0)
    logs = []
    for parity in range(2):
        theta, sketch, pay_a, pay_b = theta_call(a, b, proj, gates)
        a, log, *more = mid_call(pay_a, pay_b, sketch, theta, parity, parity + 1)
        b = more[0] if more else None
        logs.append(log)
    odd = lax.axis_index("site") % 2 == 1
    log = jnp.where(odd, logs[1], logs[0])
    return a.reshape(1, 32, PHYS, CHI), log[0, 0:1]


def solution(mesh):
    return jax.shard_map(
        shards,
        mesh=mesh,
        in_specs=(P("site", "bond", None, None), P("site", None, None), P()),
        out_specs=(P("site", "bond", None, None), P("site")),
        check_vma=False,
    )
```

```python
import functools
import math

import jax
import jax.numpy as jnp
from jax import lax
from jax.experimental import pallas as pl
from jax.experimental.pallas import tpu as pltpu
from jax.sharding import PartitionSpec as P

PHYS = 8
CHI = 512
epsilon = 1e-06
MESH = pl.DeviceIdType.MESH
HI = lax.Precision.HIGHEST
F32 = jnp.float32
BF16 = jnp.bfloat16
VMEM = pl.BlockSpec(memory_space=pltpu.VMEM)
ANY = pl.BlockSpec(memory_space=pl.ANY)
VLIM = 56 << 20


def params(cid=None):
    if cid is None:
        return pltpu.CompilerParams(vmem_limit_bytes=VLIM)
    return pltpu.CompilerParams(
        collective_id=cid, has_side_effects=True, vmem_limit_bytes=VLIM
    )


def place():
    s = lax.axis_index("site")
    b = lax.axis_index("bond")
    return s, b // 4, (b // 2) % 2, b % 2


def bond(x, y, c):
    return (x * 2 + y) * 2 + c


def greet(sends_to_me, count):
    barrier = pltpu.get_barrier_semaphore()
    for dev in sends_to_me:
        pl.semaphore_signal(barrier, inc=1, device_id=dev, device_id_type=MESH)
    pl.semaphore_wait(barrier, count)


def swap_rows(value, inner):
    n = value.shape[0]
    ri = lax.broadcasted_iota(jnp.int32, (n, n), 0)
    ci = lax.broadcasted_iota(jnp.int32, (n, n), 1)
    outer = n // inner
    perm = jnp.where(ci == (ri % outer) * inner + ri // outer, 1.0, 0.0).astype(BF16)
    return jnp.dot(perm, value, preferred_element_type=F32).astype(BF16)


def rcopy(src, dst, ssem, rsem, dev):
    return pltpu.make_async_remote_copy(
        src_ref=src, dst_ref=dst, send_sem=ssem, recv_sem=rsem,
        device_id=dev, device_id_type=MESH,
    )


class Ring:
    def __init__(self, out, sems, s, x, y, c, h):
        self.out, self.c = out, c
        self.ys, self.yr, self.xs, self.xr, self.cs, self.cr = sems
        self.x, self.h = x, h
        self.xp, self.xm, self.x2 = (x + 1) % 4, (x + 3) % 4, (x + 2) % 4
        self.hn = 1 - h
        self.y_dev = (s, bond(x, 1 - y, c))
        self.xp_dev = (s, bond(self.xp, y, c))
        self.xm_dev = (s, bond(self.xm, y, c))
        self.c_dev = (s, bond(x, y, 1 - c))
        self.partners = [self.y_dev, self.xp_dev, self.xm_dev, self.c_dev]
        self.started, self.core, self.ysend = [], [], []

    def slot(self, xx, yy, k):
        return self.out.at[self.c * 8 + xx * 2 + yy, pl.ds(128 * k, 128)]

    def send(self, ref, ss, rs, dev):
        d = rcopy(ref, ref, ss, rs, dev)
        d.start()
        self.started.append(d)
        return d

    def to_core(self, xx, yy, k):
        i = len(self.core)
        ref = self.slot(xx, yy, k)
        self.core.append(self.send(ref, self.cs.at[i], self.cr.at[i], self.c_dev))

    def home(self, k):
        ref = self.slot(self.x, self.h, k)
        self.ysend.append(self.send(ref, self.ys.at[k], self.yr.at[k], self.y_dev))
        for i, dev in enumerate((self.xp_dev, self.xm_dev)):
            self.send(ref, self.xs.at[i, 0, k], self.xr.at[i, 0, k], dev)
        self.to_core(self.x, self.h, k)

    def arrived(self, i, j, k, xx, yy, part):
        ref = self.slot(xx, yy, part)
        pltpu.make_async_copy(ref, ref, self.xr.at[i, j, k]).wait()

    def rest(self):
        x, h, hn, xp, xm, x2 = self.x, self.h, self.hn, self.xp, self.xm, self.x2
        xs, xr = self.xs, self.xr
        for k in range(2):
            self.ysend[k].wait_recv()
            for i, dev in enumerate((self.xp_dev, self.xm_dev)):
                self.send(self.slot(x, hn, k), xs.at[i, 1, k], xr.at[i, 1, k], dev)
            self.to_core(x, hn, k)
        for j, yy in ((0, h), (1, hn)):
            for k in range(2):
                self.arrived(0, j, k, xm, yy, k)
                if k == 0:
                    self.send(self.slot(xm, yy, 0), xs.at[0, 2, j], xr.at[0, 2, j], self.xp_dev)
                self.to_core(xm, yy, k)
                self.arrived(1, j, k, xp, yy, k)
                if k == 1:
                    self.send(self.slot(xp, yy, 1), xs.at[1, 2, j], xr.at[1, 2, j], self.xm_dev)
                self.to_core(xp, yy, k)
        for j, yy in ((0, h), (1, hn)):
            self.arrived(0, 2, j, x2, yy, 0)
            self.to_core(x2, yy, 0)
            self.arrived(1, 2, j, x2, yy, 1)
            self.to_core(x2, yy, 1)
        for d in self.core:
            d.wait_recv()

    def drain(self):
        for d in self.started:
            d.wait_send()


def ring_sems():
    sem = pltpu.SemaphoreType.DMA
    return [sem((2,)), sem((2,)), sem((2, 3, 2)), sem((2, 3, 2)), sem((16,)), sem((16,))]


def seams(s, x, y, c):
    h = (y + (s % 8) // 7) % 2
    to_left = ((s + 15) % 16, bond(x, (y + ((s + 7) % 8) // 7) % 2, c))
    from_right = ((s + 1) % 16, bond(x, h, c))
    return h, to_left, from_right


def gather_kernel(mine, out, own, zs, zr, *sems):
    s, x, y, c = place()
    h, to_left, from_right = seams(s, x, y, c)
    ring = Ring(out, sems, s, x, y, c, h)
    own[...] = swap_rows(mine[...], PHYS)
    greet([from_right] + ring.partners, 5)
    z = []
    for k in range(2):
        d = rcopy(
            own.at[pl.ds(128 * k, 128)], out.at[c * 8 + x * 2 + y, pl.ds(128 * k, 128)],
            zs.at[k], zr.at[k], to_left,
        )
        d.start()
        z.append(d)
    for k in range(2):
        z[k].wait_recv()
        ring.home(k)
    ring.rest()
    for d in z:
        d.wait_send()
    ring.drain()


def gather(own, cid):
    sem = pltpu.SemaphoreType.DMA
    return pl.pallas_call(
        gather_kernel,
        name="gather%d" % cid,
        out_shape=jax.ShapeDtypeStruct((16, 256, CHI), BF16),
        in_specs=[VMEM],
        out_specs=ANY,
        scratch_shapes=[pltpu.VMEM((256, CHI), BF16), sem((2,)), sem((2,))] + ring_sems(),
        compiler_params=params(cid),
    )(own)


BLOCKS = [(0, 0), (1, 0), (1, 1), (2, 0), (2, 1), (2, 2), (3, 0), (3, 1), (3, 2), (3, 3)]


def theta_kernel(a, b, proj_in, gates, theta, sketch, pay_a, pay_b, raw, proj, proj_sem):
    load = pltpu.make_async_copy(proj_in, proj, proj_sem)
    load.start()
    a_val = a[...]

    def raw_step(t, _):
        cols = pl.ds(pl.multiple_of(t * CHI, CHI), CHI)
        rows = pl.ds(pl.multiple_of(t * 32, 32), 32)
        acc = None
        for c in range(2):
            slots = [(i % 2) * 8 + i // 2 for i in range(8 * c, 8 * c + 8)]
            if len(b.shape) == 3:
                part = jnp.concatenate([b[i, rows, :] for i in slots], axis=0)
            else:
                part = jnp.concatenate(
                    [jnp.concatenate([b[k, i, rows, :] for i in slots], axis=0) for k in range(4)],
                    axis=1,
                )
            term = jnp.dot(a_val[:, c * 256:(c + 1) * 256], part, preferred_element_type=F32)
            acc = term if acc is None else acc + term
        raw[:, cols] = acc
        return 0

    lax.fori_loop(0, PHYS, raw_step, 0, unroll=2)
    gate = gates[lax.axis_index("site")]
    g_hi = gate.astype(BF16)
    g_lo = (gate - g_hi.astype(F32)).astype(BF16)
    g_hi, g_lo = [
        swap_rows(swap_rows(g, 8).astype(F32).T.astype(BF16), 8).astype(F32).T.astype(BF16)
        for g in (g_hi, g_lo)
    ]
    g3 = jnp.concatenate([g_hi, g_hi, g_lo], axis=1)

    def gate_step(i, ss):
        halves = []
        for e in range(2):
            rows = pl.ds(pl.multiple_of(i * 16, 16) + 8 * e, 8)
            xr = jnp.concatenate(
                [raw[rows, t * CHI:(t + 1) * CHI] for t in range(PHYS)], axis=0
            )
            hi = xr.astype(BF16)
            lo = (xr - hi.astype(F32)).astype(BF16)
            x3 = jnp.concatenate([hi, lo, hi], axis=0)
            g = jnp.dot(g3, x3, preferred_element_type=F32)
            for v in range(PHYS):
                gv = g[v * 8:(v + 1) * 8, :]
                ss = ss + gv * gv
            halves.append(g)
        rows = pl.ds(pl.multiple_of(i * 16, 16), 16)
        for v in range(PHYS):
            pair = jnp.concatenate([h[v * 8:(v + 1) * 8, :] for h in halves], axis=0)
            theta[rows, v * CHI:(v + 1) * CHI] = pair.astype(BF16)
        return ss

    ss = lax.fori_loop(0, 16, gate_step, jnp.zeros((8, CHI), F32), unroll=4)
    ss = (ss[:, 0:128] + ss[:, 128:256]) + (ss[:, 256:384] + ss[:, 384:512])
    load.wait()
    sk = jnp.dot(theta[...], proj[...], preferred_element_type=F32)
    sketch[...] = sk
    skt = sk.T
    for n, (bi, bj) in enumerate(BLOCKS):
        blk = lax.dot_general(
            skt[bi * 128:(bi + 1) * 128, :], sk[:, bj * 128:(bj + 1) * 128],
            (((1,), (0,)), ((), ())), precision=HI, preferred_element_type=F32,
        )
        if n == 0:
            for p in range(16):
                pay_a[p, 0:8, :] = blk[8 * p:8 * p + 8, :]
            continue
        r = 128 * (n - 1)
        while r < 128 * n:
            p, o = r // 72, r % 72
            e = min(72 - o, 128 * n - r)
            pay_b[p, o:o + e, :] = blk[r - 128 * (n - 1):r - 128 * (n - 1) + e, :]
            r += e
    for p in range(16):
        pay_a[p, 8:16, :] = ss


def theta_call(a, b, proj, gates):
    return pl.pallas_call(
        theta_kernel,
        name="theta",
        out_shape=[
            jax.ShapeDtypeStruct((256, PHYS * CHI), BF16),
            jax.ShapeDtypeStruct((256, CHI), F32),
            jax.ShapeDtypeStruct((16, 16, 128), F32),
            jax.ShapeDtypeStruct((16, 72, 128), F32),
        ],
        in_specs=[VMEM, VMEM, ANY, VMEM],
        out_specs=[VMEM] * 4,
        scratch_shapes=[
            pltpu.VMEM((256, PHYS * CHI), F32), pltpu.VMEM((PHYS * CHI, CHI), BF16),
            pltpu.SemaphoreType.DMA,
        ],
        compiler_params=params(),
    )(a, b, proj, gates)


class Sum:
    def __init__(self, pay, half, rb0, rb1, out, sems, c, me, c_dev, devs, sent):
        self.pay, self.half, self.rb0, self.rb1, self.out = pay, half, rb0, rb1, out
        self.sems, self.c, self.me, self.c_dev, self.devs = sems, c, me, c_dev, devs
        self.sent, self.cores = sent, []

    def send(self, src, dst, i, k, dev):
        d = rcopy(src, dst, self.sems[2 * i].at[k], self.sems[2 * i + 1].at[k], dev)
        d.start()
        self.sent.append(d)
        return d

    def begin(self):
        self.core = self.send(self.pay.at[pl.ds((1 - self.c) * 8, 8)], self.rb0, 0, 0, self.c_dev)

    def scatter(self):
        self.core.wait_recv()
        self.half[...] = self.pay[pl.ds(self.c * 8, 8)] + self.rb0[...]
        self.parts = [
            self.send(self.half.at[(self.me + k + 1) % 8], self.rb1.at[k], 1, k, dev)
            for k, dev in enumerate(self.devs)
        ]

    def spread(self):
        for d in self.parts:
            d.wait_recv()
        t = [self.rb1[k] for k in range(7)]
        slot = self.c * 8 + self.me
        self.out[slot] = ((self.half[self.me] + t[0]) + (t[1] + t[2])) + (
            (t[3] + t[4]) + (t[5] + t[6]))
        ref = self.out.at[slot]
        self.wide = [self.send(ref, ref, 2, k, dev) for k, dev in enumerate(self.devs)]
        self.cores.append(self.send(ref, ref, 3, 7, self.c_dev))

    def forward(self):
        for k in range(7):
            self.wide[k].wait_recv()
            ref = self.out.at[self.c * 8 + (self.me + 7 - k) % 8]
            self.cores.append(self.send(ref, ref, 3, k, self.c_dev))

    def finish(self):
        for d in self.cores:
            d.wait_recv()


def sum_scratch(rows):
    sem = pltpu.SemaphoreType.DMA
    return [
        pltpu.VMEM((8, rows, 128), F32), pltpu.VMEM((8, rows, 128), F32),
        pltpu.VMEM((7, rows, 128), F32), pltpu.VMEM((16, rows, 128), F32),
        sem((1,)), sem((1,)), sem((7,)), sem((7,)), sem((7,)), sem((7,)), sem((8,)), sem((8,)),
    ]


def bl(v, k):
    return jnp.broadcast_to(v[:, k:k + 1], (8, 128))


def bs(v, j):
    return jnp.broadcast_to(v[j:j + 1, :], (8, 128))


def leaf(rows, hook):
    lane = lax.broadcasted_iota(jnp.int32, (8, 128), 1)
    sub = lax.broadcasted_iota(jnp.int32, (8, 128), 0)
    rows = list(rows)
    out = []
    n = len(rows)
    for p in range(n):
        m_p = rows[p]
        c = [bl(m_p, 8 * p + v) for v in range(8)]
        pc = (lane >= 8 * p) & (lane < 8 * p + 8)
        m_p = jnp.where(pc, jnp.where(lane - 8 * p == sub, 1.0, 0.0), m_p)
        fwd = m_p
        diag = None
        for j in range(8):
            d = bs(c[j], j)
            isj = sub == j
            mult = jnp.where(isj, 0.0, c[j] * (1.0 / d))
            if j:
                diag = jnp.where(isj, d, diag)
                fwd = jnp.where(isj, m_p, fwd)
            else:
                diag = d
            for v in range(j + 1, 8):
                c[v] = c[v] - mult * bs(c[v], j)
            m_p = m_p - mult * bs(m_p, j)
        out.append(jnp.where(lane < 8 * p + 8, fwd * lax.rsqrt(diag), 0.0))
        if p == n - 1:
            break
        yy = m_p * (1.0 / diag)
        yb = [bs(yy, v) for v in range(8)]
        for q in range(p + 1, n):
            t = [bl(rows[q], 8 * p + v) * yb[v] for v in range(8)]
            tot = ((t[0] + t[1]) + (t[2] + t[3])) + ((t[4] + t[5]) + (t[6] + t[7]))
            rows[q] = jnp.where(pc, 0.0, rows[q]) - tot
        hook(p)
    return out


def dott(a, b):
    return lax.dot_general(
        a, b, (((1,), (1,)), ((), ())), precision=HI, preferred_element_type=F32
    )


def dotn(a, b):
    return lax.dot_general(
        a, b, (((1,), (0,)), ((), ())), precision=HI, preferred_element_type=F32
    )


def unpack_rest(pay, a):
    for n, (bi, bj) in enumerate(BLOCKS[1:]):
        r = 128 * n
        while r < 128 * n + 128:
            p, o = r // 72, r % 72
            e = min(72 - o, 128 * n + 128 - r)
            q = bi * 128 + r - 128 * n
            a[q:q + e, bj * 128:(bj + 1) * 128] = pay[p, o:o + e, :]
            r += e


def mid_kernel(parity, *refs):
    first = parity == 0
    refs = list(refs)
    pay_a, pay_b, sketch, theta, left, log = refs[:6]
    refs = refs[6:]
    if first:
        bout, lp, zs, zr, gxs, gxr, gcs, gcr = refs[:1] + refs[-7:]
        refs = refs[1:-7]
    a, linv, part, rbc, rby, rbx, rby2, rbx2, fin, rcol, lnt = refs[:11]
    cs, cr, ds, dr, as_, ar = refs[11:17]
    scr_a, scr_b = refs[17:29], refs[29:41]

    s, x, y, c = place()
    is_left = s % 2 == parity
    _, to_left, from_right = seams(s, x, y, c)
    c_dev = (s, bond(x, y, 1 - c))
    right, before = (s + 1) % 16, (s + 15) % 16
    others = [(x * 2 + y + k) % 8 for k in range(1, 8)]
    greet(
        [c_dev] + [(s, bond(q // 2, q % 2, c)) for q in others]
        + [(before, q) for q in range(16)] + ([from_right] if first else []),
        25 if first else 24,
    )
    me = c * 8 + y * 4 + x
    y_dev = (s, bond(x, 1 - y, c))
    x_devs = [(s, bond((x + k) % 4, y, c)) for k in range(1, 4)]
    root = math.sqrt(PHYS * CHI)

    @pl.when(is_left)
    def _():
        sent = []

        def send(src, dst, ss, rs, dev):
            d = rcopy(src, dst, ss, rs, dev)
            d.start()
            sent.append(d)
            return d

        devs = [(s, bond(q // 2, q % 2, c)) for q in others]
        sums = [
            Sum(pay, *scr[:4], scr[4:], c, x * 2 + y, c_dev, devs, sent)
            for pay, scr in ((pay_a, scr_a), (pay_b, scr_b))
        ]
        for f in ("begin", "scatter", "spread"):
            for v in sums:
                getattr(v, f)()
        sums[0].forward()
        sums[0].finish()
        gram = scr_a[3]
        total = jnp.sum(jnp.sum(gram[0, 8:16, :], axis=0, keepdims=True), axis=1, keepdims=True)
        mean_square = total * (1.0 / (CHI * PHYS * PHYS * CHI)) + epsilon
        log[...] = jnp.broadcast_to(0.5 * jnp.log(mean_square), (8, 128))
        scale = lax.rsqrt(mean_square) * (1.0 / root)
        for p in range(16):
            a[8 * p:8 * p + 8, 0:128] = gram[p, 0:8, :]
        core, hops = {}, {}

        def columns(b):
            o = b * 128
            if b:
                linv[o:o + 128, :o] = -dotn(
                    linv[o:o + 128, o:o + 128], dotn(a[o:o + 128, :o], linv[:o, :o])
                )
            ln = (dott(sketch[:, :o + 128], linv[o:o + 128, :o + 128]) * root).astype(BF16)
            left[:, o:o + 128] = ln
            if first:
                lp[b] = swap_rows(ln, PHYS)
                send(lp.at[b], bout.at[b, c * 8 + x * 2 + y], zs.at[b], zr.at[b], to_left)
            lnt[...] = ln.astype(F32).T.astype(BF16)

        def partial(b, t):
            blk = jnp.dot(
                lnt[...], theta[:, t * CHI:(t + 1) * CHI], preferred_element_type=F32
            )
            blk = (blk * scale).astype(BF16)
            part[b, 2 * t] = blk[:, 0:256]
            part[b, 2 * t + 1] = blk[:, 256:512]

        def to_core(b):
            core[b] = send(
                part.at[b, pl.ds((1 - c) * 8, 8)], rbc.at[b], cs.at[b], cr.at[b], c_dev
            )

        lo, hi = pl.ds(0, 64), pl.ds(64, 64)

        def hop(b, i, src, dst, dev):
            hops[b, i] = send(src, dst, ds.at[b, i], dr.at[b, i], dev)

        def step_a(b):
            core[b].wait_recv()
            half = part[b, pl.ds(c * 8, 8)].astype(F32) + rbc[b].astype(F32)
            part[b, pl.ds(c * 8, 8)] = half.astype(BF16)
            hop(b, 0, part.at[b, pl.ds(c * 8 + (1 - y) * 4, 4), lo], rby.at[b], y_dev)
            for k in range(3):
                xx = (x + k + 1) % 4
                for yy in range(2):
                    hop(b, 1 + 2 * k + yy, part.at[b, c * 8 + yy * 4 + xx, hi],
                        rbx.at[b, k, yy], x_devs[k])

        def step_b(b):
            hops[b, 0].wait_recv()
            row = pl.ds(c * 8 + y * 4, 4)
            part[b, row, lo] = (part[b, row, lo].astype(F32) + rby[b].astype(F32)).astype(BF16)
            for k in range(3):
                hop(b, 7 + k, part.at[b, c * 8 + y * 4 + (x + k + 1) % 4, lo],
                    rbx2.at[b, k], x_devs[k])
            for i in range(1, 7):
                hops[b, i].wait_recv()
            for yy in range(2):
                i = c * 8 + yy * 4 + x
                tot = (part[b, i, hi].astype(F32) + rbx[b, 0, yy].astype(F32)) + (
                    rbx[b, 1, yy].astype(F32) + rbx[b, 2, yy].astype(F32))
                part[b, i, hi] = tot.astype(BF16)
            hop(b, 10, part.at[b, c * 8 + (1 - y) * 4 + x, hi], rby2.at[b], y_dev)

        def step_d(b):
            for i in range(7, 11):
                hops[b, i].wait_recv()
            tot = (part[b, me, lo].astype(F32) + rbx2[b, 0].astype(F32)) + (
                rbx2[b, 1].astype(F32) + rbx2[b, 2].astype(F32))
            fin[b, lo] = tot.astype(BF16)
            fin[b, hi] = (part[b, me, hi].astype(F32) + rby2[b].astype(F32)).astype(BF16)
            for i in range(4):
                send(
                    fin.at[b, pl.ds(32 * i, 32)], rcol.at[me], as_.at[b, i], ar.at[me],
                    (right, 4 * b + i),
                )

        def update(b):
            o = b * 128
            if b < 2:
                rest = slice(o + 256, CHI)
                lb = dott(a[rest, o:o + 128], linv[o:o + 128, o:o + 128])
                a[rest, o:o + 128] = lb
                a[rest, o + 128:o + 256] = a[rest, o + 128:o + 256] - dott(
                    lb, a[o + 128:o + 256, o:o + 128])
                a[rest, rest] = a[rest, rest] - dott(lb, lb)

        plan = {0: {8: [lambda: sums[1].forward()]}}
        for b in range(1, 4):
            steps = {0: [functools.partial(columns, b - 1)]}
            for t in range(PHYS):
                steps.setdefault(1 + t // 2, []).append(functools.partial(partial, b - 1, t))
            steps[5] = [functools.partial(to_core, b - 1)]
            steps[6] = [functools.partial(update, b - 1)]
            steps[13] = [functools.partial(step_a, b - 1)]
            if b > 1:
                steps[9] = [functools.partial(step_b, b - 2)]
            if b > 2:
                steps[7] = [functools.partial(step_d, b - 3)]
            plan[b] = steps
        for b in range(4):
            o = b * 128

            def hook(p, b=b):
                for f in plan[b].get(p, ()):
                    f()

            linv[o:o + 128, o:o + 128] = jnp.concatenate(
                leaf([a[o + 8 * q:o + 8 * q + 8, o:o + 128] for q in range(16)], hook), 0
            )
            if b == 0:
                sums[1].finish()
                unpack_rest(scr_b[3], a)
            if b < 3:
                linv[o:o + 128, o + 128:] = jnp.zeros((128, CHI - o - 128), F32)
                after = slice(o + 128, o + 256)
                lb = dott(a[after, o:o + 128], linv[o:o + 128, o:o + 128])
                a[after, o:o + 128] = lb
                a[after, after] = a[after, after] - dott(lb, lb)
        columns(3)
        for t in range(PHYS):
            partial(3, t)
        to_core(3)
        step_d(1)
        step_b(2)
        step_a(3)
        step_d(2)
        step_b(3)
        step_d(3)
        for d in sent:
            d.wait_send()

    @pl.when(jnp.logical_not(is_left))
    def _():
        if first:
            seam = (s % 8) // 7
            sent, cores = [], []

            def slot(b, k, other):
                yy = (y + other + seam) % 2
                return bout.at[b, c * 8 + ((x + 4 - k) % 4) * 2 + yy]

            def send(b, i, ref, dev):
                d = rcopy(ref, ref, gxs.at[b, i], gxr.at[b, i], dev)
                d.start()
                sent.append(d)

            def to_sibling(b, i, ref):
                d = rcopy(ref, ref, gcs.at[b, i], gcr.at[b, i], c_dev)
                d.start()
                sent.append(d)
                cores.append(d)

            def here(ref, rs):
                pltpu.make_async_copy(ref, ref, rs).wait()

            lo, hi = pl.ds(0, 128), pl.ds(128, 128)

            def one(b):
                ref = slot(b, 0, 0)
                here(ref, zr.at[b])
                send(b, 0, ref.at[lo], y_dev)
                for k in range(3):
                    send(b, 1 + k, ref.at[hi], x_devs[k])
                for k in range(3):
                    send(b, 4 + k, ref.at[lo], x_devs[k])
                send(b, 13, ref.at[hi], y_dev)
                to_sibling(b, 0, ref)

            def two(b):
                ref = slot(b, 0, 1)
                here(ref.at[lo], gxr.at[b, 0])
                for k in range(3):
                    send(b, 7 + k, ref.at[lo], x_devs[k])
                for k in range(3):
                    ref = slot(b, k + 1, 0)
                    here(ref.at[hi], gxr.at[b, 1 + k])
                    send(b, 10 + k, ref.at[hi], y_dev)

            def three(b):
                for k in range(3):
                    ref = slot(b, k + 1, 0)
                    here(ref.at[lo], gxr.at[b, 4 + k])
                    to_sibling(b, 1 + k, ref)
                ref = slot(b, 0, 1)
                here(ref.at[hi], gxr.at[b, 13])
                to_sibling(b, 4, ref)
                for k in range(3):
                    ref = slot(b, k + 1, 1)
                    here(ref.at[lo], gxr.at[b, 7 + k])
                    here(ref.at[hi], gxr.at[b, 10 + k])
                    to_sibling(b, 5 + k, ref)

            one(0)
            two(0)
            for b in range(1, 4):
                one(b)
                three(b - 1)
                two(b)
            three(3)
            for d in cores:
                d.wait_recv()
            for d in sent:
                d.wait_send()
        for q in range(16):
            pltpu.make_async_copy(rcol.at[q], rcol.at[q], ar.at[q]).wait()
        rows = jnp.concatenate(
            [jnp.concatenate([rcol[2 * t], rcol[2 * t + 1]], axis=1) for t in range(PHYS)], axis=0
        )
        left[...] = swap_rows(rows, 32)


def mid_call(pay_a, pay_b, sketch, theta, parity, cid):
    sem = pltpu.SemaphoreType.DMA
    first = parity == 0
    outs = [
        jax.ShapeDtypeStruct((256, CHI), BF16),
        jax.ShapeDtypeStruct((8, 128), F32),
    ]
    scratch = [
        pltpu.VMEM((CHI, CHI), F32), pltpu.VMEM((CHI, CHI), F32),
        pltpu.VMEM((4, 16, 128, 256), BF16), pltpu.VMEM((4, 8, 128, 256), BF16),
        pltpu.VMEM((4, 4, 64, 256), BF16), pltpu.VMEM((4, 3, 2, 64, 256), BF16),
        pltpu.VMEM((4, 64, 256), BF16), pltpu.VMEM((4, 3, 64, 256), BF16),
        pltpu.VMEM((4, 128, 256), BF16),
        pltpu.VMEM((16, 32, 256), BF16), pltpu.VMEM((128, 256), BF16),
        sem((4,)), sem((4,)), sem((4, 11)), sem((4, 11)), sem((4, 4)), sem((16,)),
    ] + sum_scratch(16) + sum_scratch(72)
    if first:
        outs.append(jax.ShapeDtypeStruct((4, 16, 256, 128), BF16))
        scratch += [
            pltpu.VMEM((4, 256, 128), BF16), sem((4,)), sem((4,)),
            sem((4, 14)), sem((4, 14)), sem((4, 8)), sem((4, 8)),
        ]
    return pl.pallas_call(
        functools.partial(mid_kernel, parity),
        name="mid%d" % cid,
        out_shape=outs,
        in_specs=[VMEM] * 4,
        out_specs=[VMEM] * len(outs),
        scratch_shapes=scratch,
        compiler_params=params(cid),
    )(pay_a, pay_b, sketch, theta)


def shards(mps, projection, gates):
    proj = projection[0]
    a = mps[0].reshape(256, CHI)
    b = gather(a, 0)
    logs = []
    for parity in range(2):
        theta, sketch, pay_a, pay_b = theta_call(a, b, proj, gates)
        a, log, *more = mid_call(pay_a, pay_b, sketch, theta, parity, parity + 1)
        b = more[0] if more else None
        logs.append(log)
    odd = lax.axis_index("site") % 2 == 1
    log = jnp.where(odd, logs[1], logs[0])
    return a.reshape(1, 32, PHYS, CHI), log[0, 0:1]


def solution(mesh):
    return jax.shard_map(
        shards,
        mesh=mesh,
        in_specs=(P("site", "bond", None, None), P("site", None, None), P()),
        out_specs=(P("site", "bond", None, None), P("site")),
        check_vma=False,
    )
```

```python
import functools
import math

import jax
import jax.numpy as jnp
from jax import lax
from jax.experimental import pallas as pl
from jax.experimental.pallas import tpu as pltpu
from jax.sharding import PartitionSpec as P

PHYS = 8
CHI = 512
epsilon = 1e-06
MESH = pl.DeviceIdType.MESH
HI = lax.Precision.HIGHEST
F32 = jnp.float32
BF16 = jnp.bfloat16
VMEM = pl.BlockSpec(memory_space=pltpu.VMEM)
ANY = pl.BlockSpec(memory_space=pl.ANY)
VLIM = 56 << 20


def params(cid=None):
    if cid is None:
        return pltpu.CompilerParams(vmem_limit_bytes=VLIM)
    return pltpu.CompilerParams(
        collective_id=cid, has_side_effects=True, vmem_limit_bytes=VLIM
    )


def place():
    s = lax.axis_index("site")
    b = lax.axis_index("bond")
    return s, b // 4, (b // 2) % 2, b % 2


def bond(x, y, c):
    return (x * 2 + y) * 2 + c


def greet(sends_to_me, count):
    barrier = pltpu.get_barrier_semaphore()
    for dev in sends_to_me:
        pl.semaphore_signal(barrier, inc=1, device_id=dev, device_id_type=MESH)
    pl.semaphore_wait(barrier, count)


def swap_rows(value, inner):
    n = value.shape[0]
    ri = lax.broadcasted_iota(jnp.int32, (n, n), 0)
    ci = lax.broadcasted_iota(jnp.int32, (n, n), 1)
    outer = n // inner
    perm = jnp.where(ci == (ri % outer) * inner + ri // outer, 1.0, 0.0).astype(BF16)
    return jnp.dot(perm, value, preferred_element_type=F32).astype(BF16)


def rcopy(src, dst, ssem, rsem, dev):
    return pltpu.make_async_remote_copy(
        src_ref=src, dst_ref=dst, send_sem=ssem, recv_sem=rsem,
        device_id=dev, device_id_type=MESH,
    )


class Ring:
    def __init__(self, out, sems, s, x, y, c, h):
        self.out, self.c = out, c
        self.ys, self.yr, self.xs, self.xr, self.cs, self.cr = sems
        self.x, self.h = x, h
        self.xp, self.xm, self.x2 = (x + 1) % 4, (x + 3) % 4, (x + 2) % 4
        self.hn = 1 - h
        self.y_dev = (s, bond(x, 1 - y, c))
        self.xp_dev = (s, bond(self.xp, y, c))
        self.xm_dev = (s, bond(self.xm, y, c))
        self.c_dev = (s, bond(x, y, 1 - c))
        self.partners = [self.y_dev, self.xp_dev, self.xm_dev, self.c_dev]
        self.started, self.core, self.ysend = [], [], []

    def slot(self, xx, yy, k):
        return self.out.at[self.c * 8 + xx * 2 + yy, pl.ds(64 * k, 64)]

    def send(self, ref, ss, rs, dev):
        d = rcopy(ref, ref, ss, rs, dev)
        d.start()
        self.started.append(d)
        return d

    def to_core(self, xx, yy, k):
        i = len(self.core)
        ref = self.slot(xx, yy, k)
        self.core.append(self.send(ref, self.cs.at[i], self.cr.at[i], self.c_dev))

    def home(self, k):
        ref = self.slot(self.x, self.h, k)
        self.ysend.append(self.send(ref, self.ys.at[k], self.yr.at[k], self.y_dev))
        for i, dev in enumerate((self.xp_dev, self.xm_dev)):
            self.send(ref, self.xs.at[i, 0, k], self.xr.at[i, 0, k], dev)
        self.to_core(self.x, self.h, k)

    def arrived(self, i, j, k, xx, yy, part):
        ref = self.slot(xx, yy, part)
        pltpu.make_async_copy(ref, ref, self.xr.at[i, j, k]).wait()

    def rest(self):
        x, h, hn, xp, xm, x2 = self.x, self.h, self.hn, self.xp, self.xm, self.x2
        xs, xr = self.xs, self.xr
        for k in range(4):
            self.ysend[k].wait_recv()
            for i, dev in enumerate((self.xp_dev, self.xm_dev)):
                self.send(self.slot(x, hn, k), xs.at[i, 1, k], xr.at[i, 1, k], dev)
            self.to_core(x, hn, k)
        for j, yy in ((0, h), (1, hn)):
            for k in range(4):
                for i, (xx, dev) in enumerate(((xm, self.xp_dev), (xp, self.xm_dev))):
                    self.arrived(i, j, k, xx, yy, k)
                    if k // 2 == i:
                        self.send(self.slot(xx, yy, k), xs.at[i, 2 + j, k], xr.at[i, 2 + j, k], dev)
                    self.to_core(xx, yy, k)
        for j, yy in ((0, h), (1, hn)):
            for k in range(4):
                self.arrived(k // 2, 2 + j, k, x2, yy, k)
                self.to_core(x2, yy, k)
        for d in self.core:
            d.wait_recv()

    def drain(self):
        for d in self.started:
            d.wait_send()


def ring_sems():
    sem = pltpu.SemaphoreType.DMA
    return [sem((4,)), sem((4,)), sem((2, 4, 4)), sem((2, 4, 4)), sem((32,)), sem((32,))]


def seams(s, x, y, c):
    h = (y + (s % 8) // 7) % 2
    to_left = ((s + 15) % 16, bond(x, (y + ((s + 7) % 8) // 7) % 2, c))
    from_right = ((s + 1) % 16, bond(x, h, c))
    return h, to_left, from_right


def gather_kernel(mine, out, own, zs, zr, *sems):
    s, x, y, c = place()
    h, to_left, from_right = seams(s, x, y, c)
    ring = Ring(out, sems, s, x, y, c, h)
    own[...] = swap_rows(mine[...], PHYS)
    greet([from_right] + ring.partners, 5)
    z = []
    for k in range(4):
        d = rcopy(
            own.at[pl.ds(64 * k, 64)], out.at[c * 8 + x * 2 + y, pl.ds(64 * k, 64)],
            zs.at[k], zr.at[k], to_left,
        )
        d.start()
        z.append(d)
    for k in range(4):
        z[k].wait_recv()
        ring.home(k)
    ring.rest()
    for d in z:
        d.wait_send()
    ring.drain()


def gather(own, cid):
    sem = pltpu.SemaphoreType.DMA
    return pl.pallas_call(
        gather_kernel,
        name="gather%d" % cid,
        out_shape=jax.ShapeDtypeStruct((16, 256, CHI), BF16),
        in_specs=[VMEM],
        out_specs=ANY,
        scratch_shapes=[pltpu.VMEM((256, CHI), BF16), sem((4,)), sem((4,))] + ring_sems(),
        compiler_params=params(cid),
    )(own)


BLOCKS = [(0, 0), (1, 0), (1, 1), (2, 0), (2, 1), (2, 2), (3, 0), (3, 1), (3, 2), (3, 3)]


def theta_kernel(a, b, proj_in, gates, theta, sketch, pay_a, pay_b, raw, proj, proj_sem):
    load = pltpu.make_async_copy(proj_in, proj, proj_sem)
    load.start()
    a_val = a[...]

    def raw_step(t, _):
        cols = pl.ds(pl.multiple_of(t * CHI, CHI), CHI)
        rows = pl.ds(pl.multiple_of(t * 32, 32), 32)
        acc = None
        for c in range(2):
            slots = [(i % 2) * 8 + i // 2 for i in range(8 * c, 8 * c + 8)]
            if len(b.shape) == 3:
                part = jnp.concatenate([b[i, rows, :] for i in slots], axis=0)
            else:
                part = jnp.concatenate(
                    [jnp.concatenate([b[k, i, rows, :] for i in slots], axis=0) for k in range(4)],
                    axis=1,
                )
            term = jnp.dot(a_val[:, c * 256:(c + 1) * 256], part, preferred_element_type=F32)
            acc = term if acc is None else acc + term
        raw[:, cols] = acc
        return 0

    lax.fori_loop(0, PHYS, raw_step, 0, unroll=2)
    gate = gates[lax.axis_index("site")]
    g_hi = gate.astype(BF16)
    g_lo = (gate - g_hi.astype(F32)).astype(BF16)
    g_hi, g_lo = [
        swap_rows(swap_rows(g, 8).astype(F32).T.astype(BF16), 8).astype(F32).T.astype(BF16)
        for g in (g_hi, g_lo)
    ]
    g3 = jnp.concatenate([g_hi, g_hi, g_lo], axis=1)

    def gate_step(i, ss):
        halves = []
        for e in range(2):
            rows = pl.ds(pl.multiple_of(i * 16, 16) + 8 * e, 8)
            xr = jnp.concatenate(
                [raw[rows, t * CHI:(t + 1) * CHI] for t in range(PHYS)], axis=0
            )
            hi = xr.astype(BF16)
            lo = (xr - hi.astype(F32)).astype(BF16)
            x3 = jnp.concatenate([hi, lo, hi], axis=0)
            g = jnp.dot(g3, x3, preferred_element_type=F32)
            for v in range(PHYS):
                gv = g[v * 8:(v + 1) * 8, :]
                ss = ss + gv * gv
            halves.append(g)
        rows = pl.ds(pl.multiple_of(i * 16, 16), 16)
        for v in range(PHYS):
            pair = jnp.concatenate([h[v * 8:(v + 1) * 8, :] for h in halves], axis=0)
            theta[rows, v * CHI:(v + 1) * CHI] = pair.astype(BF16)
        return ss

    ss = lax.fori_loop(0, 16, gate_step, jnp.zeros((8, CHI), F32), unroll=4)
    ss = (ss[:, 0:128] + ss[:, 128:256]) + (ss[:, 256:384] + ss[:, 384:512])
    load.wait()
    sk = jnp.dot(theta[...], proj[...], preferred_element_type=F32)
    sketch[...] = sk
    skt = sk.T
    for n, (bi, bj) in enumerate(BLOCKS):
        blk = lax.dot_general(
            skt[bi * 128:(bi + 1) * 128, :], sk[:, bj * 128:(bj + 1) * 128],
            (((1,), (0,)), ((), ())), precision=HI, preferred_element_type=F32,
        )
        if n == 0:
            for p in range(16):
                pay_a[p, 0:8, :] = blk[8 * p:8 * p + 8, :]
            continue
        r = 128 * (n - 1)
        while r < 128 * n:
            p, o = r // 72, r % 72
            e = min(72 - o, 128 * n - r)
            pay_b[p, o:o + e, :] = blk[r - 128 * (n - 1):r - 128 * (n - 1) + e, :]
            r += e
    for p in range(16):
        pay_a[p, 8:16, :] = ss


def theta_call(a, b, proj, gates):
    return pl.pallas_call(
        theta_kernel,
        name="theta",
        out_shape=[
            jax.ShapeDtypeStruct((256, PHYS * CHI), BF16),
            jax.ShapeDtypeStruct((256, CHI), F32),
            jax.ShapeDtypeStruct((16, 16, 128), F32),
            jax.ShapeDtypeStruct((16, 72, 128), F32),
        ],
        in_specs=[VMEM, VMEM, ANY, VMEM],
        out_specs=[VMEM] * 4,
        scratch_shapes=[
            pltpu.VMEM((256, PHYS * CHI), F32), pltpu.VMEM((PHYS * CHI, CHI), BF16),
            pltpu.SemaphoreType.DMA,
        ],
        compiler_params=params(),
    )(a, b, proj, gates)


class Sum:
    def __init__(self, pay, half, rb0, rb1, out, sems, c, me, c_dev, devs, sent):
        self.pay, self.half, self.rb0, self.rb1, self.out = pay, half, rb0, rb1, out
        self.sems, self.c, self.me, self.c_dev, self.devs = sems, c, me, c_dev, devs
        self.sent, self.cores = sent, []

    def send(self, src, dst, i, k, dev):
        d = rcopy(src, dst, self.sems[2 * i].at[k], self.sems[2 * i + 1].at[k], dev)
        d.start()
        self.sent.append(d)
        return d

    def begin(self):
        self.core = self.send(self.pay.at[pl.ds((1 - self.c) * 8, 8)], self.rb0, 0, 0, self.c_dev)

    def scatter(self):
        self.core.wait_recv()
        self.half[...] = self.pay[pl.ds(self.c * 8, 8)] + self.rb0[...]
        self.parts = [
            self.send(self.half.at[(self.me + k + 1) % 8], self.rb1.at[k], 1, k, dev)
            for k, dev in enumerate(self.devs)
        ]

    def spread(self):
        for d in self.parts:
            d.wait_recv()
        t = [self.rb1[k] for k in range(7)]
        slot = self.c * 8 + self.me
        self.out[slot] = ((self.half[self.me] + t[0]) + (t[1] + t[2])) + (
            (t[3] + t[4]) + (t[5] + t[6]))
        ref = self.out.at[slot]
        self.wide = [self.send(ref, ref, 2, k, dev) for k, dev in enumerate(self.devs)]
        self.cores.append(self.send(ref, ref, 3, 7, self.c_dev))

    def forward(self):
        for k in range(7):
            self.wide[k].wait_recv()
            ref = self.out.at[self.c * 8 + (self.me + 7 - k) % 8]
            self.cores.append(self.send(ref, ref, 3, k, self.c_dev))

    def finish(self):
        for d in self.cores:
            d.wait_recv()


def sum_scratch(rows):
    sem = pltpu.SemaphoreType.DMA
    return [
        pltpu.VMEM((8, rows, 128), F32), pltpu.VMEM((8, rows, 128), F32),
        pltpu.VMEM((7, rows, 128), F32), pltpu.VMEM((16, rows, 128), F32),
        sem((1,)), sem((1,)), sem((7,)), sem((7,)), sem((7,)), sem((7,)), sem((8,)), sem((8,)),
    ]


def bl(v, k):
    return jnp.broadcast_to(v[:, k:k + 1], (8, 128))


def bs(v, j):
    return jnp.broadcast_to(v[j:j + 1, :], (8, 128))


def leaf(rows, hook):
    lane = lax.broadcasted_iota(jnp.int32, (8, 128), 1)
    sub = lax.broadcasted_iota(jnp.int32, (8, 128), 0)
    rows = list(rows)
    out = []
    n = len(rows)
    for p in range(n):
        m_p = rows[p]
        c = [bl(m_p, 8 * p + v) for v in range(8)]
        pc = (lane >= 8 * p) & (lane < 8 * p + 8)
        m_p = jnp.where(pc, jnp.where(lane - 8 * p == sub, 1.0, 0.0), m_p)
        fwd = m_p
        diag = None
        for j in range(8):
            d = bs(c[j], j)
            isj = sub == j
            mult = jnp.where(isj, 0.0, c[j] * (1.0 / d))
            if j:
                diag = jnp.where(isj, d, diag)
                fwd = jnp.where(isj, m_p, fwd)
            else:
                diag = d
            for v in range(j + 1, 8):
                c[v] = c[v] - mult * bs(c[v], j)
            m_p = m_p - mult * bs(m_p, j)
        out.append(jnp.where(lane < 8 * p + 8, fwd * lax.rsqrt(diag), 0.0))
        if p == n - 1:
            break
        yy = m_p * (1.0 / diag)
        yb = [bs(yy, v) for v in range(8)]
        for q in range(p + 1, n):
            t = [bl(rows[q], 8 * p + v) * yb[v] for v in range(8)]
            tot = ((t[0] + t[1]) + (t[2] + t[3])) + ((t[4] + t[5]) + (t[6] + t[7]))
            rows[q] = jnp.where(pc, 0.0, rows[q]) - tot
        hook(p)
    return out


def dott(a, b):
    return lax.dot_general(
        a, b, (((1,), (1,)), ((), ())), precision=HI, preferred_element_type=F32
    )


def dotn(a, b):
    return lax.dot_general(
        a, b, (((1,), (0,)), ((), ())), precision=HI, preferred_element_type=F32
    )


def unpack_rest(pay, a):
    for n, (bi, bj) in enumerate(BLOCKS[1:]):
        r = 128 * n
        while r < 128 * n + 128:
            p, o = r // 72, r % 72
            e = min(72 - o, 128 * n + 128 - r)
            q = bi * 128 + r - 128 * n
            a[q:q + e, bj * 128:(bj + 1) * 128] = pay[p, o:o + e, :]
            r += e


def mid_kernel(parity, *refs):
    first = parity == 0
    refs = list(refs)
    pay_a, pay_b, sketch, theta, left, log = refs[:6]
    refs = refs[6:]
    if first:
        bout, lp, zs, zr, gxs, gxr, gcs, gcr = refs[:1] + refs[-7:]
        refs = refs[1:-7]
    a, linv, part, rbc, rby, rbx, rby2, rbx2, fin, rcol, lnt, ahead = refs[:12]
    cs, cr, ds, dr, as_, ar = refs[12:18]
    scr_a, scr_b = refs[18:30], refs[30:42]

    s, x, y, c = place()
    is_left = s % 2 == parity
    _, to_left, from_right = seams(s, x, y, c)
    c_dev = (s, bond(x, y, 1 - c))
    right, before = (s + 1) % 16, (s + 15) % 16
    others = [(x * 2 + y + k) % 8 for k in range(1, 8)]
    greet(
        [c_dev] + [(s, bond(q // 2, q % 2, c)) for q in others]
        + [(before, q) for q in range(16)] + ([from_right] if first else []),
        25 if first else 24,
    )
    me = c * 8 + y * 4 + x
    y_dev = (s, bond(x, 1 - y, c))
    x_devs = [(s, bond((x + k) % 4, y, c)) for k in range(1, 4)]
    root = math.sqrt(PHYS * CHI)

    @pl.when(is_left)
    def _():
        sent = []

        def send(src, dst, ss, rs, dev):
            d = rcopy(src, dst, ss, rs, dev)
            d.start()
            sent.append(d)
            return d

        devs = [(s, bond(q // 2, q % 2, c)) for q in others]
        sums = [
            Sum(pay, *scr[:4], scr[4:], c, x * 2 + y, c_dev, devs, sent)
            for pay, scr in ((pay_a, scr_a), (pay_b, scr_b))
        ]
        for f in ("begin", "scatter", "spread"):
            for v in sums:
                getattr(v, f)()
        sums[0].forward()
        sums[0].finish()
        gram = scr_a[3]
        total = jnp.sum(jnp.sum(gram[0, 8:16, :], axis=0, keepdims=True), axis=1, keepdims=True)
        mean_square = total * (1.0 / (CHI * PHYS * PHYS * CHI)) + epsilon
        log[...] = jnp.broadcast_to(0.5 * jnp.log(mean_square), (8, 128))
        scale = lax.rsqrt(mean_square) * (1.0 / root)
        for p in range(16):
            a[8 * p:8 * p + 8, 0:128] = gram[p, 0:8, :]
        core, hops = {}, {}

        def columns(b):
            o = b * 128
            if b == 3:
                ln = (dott(ahead[...], linv[o:, o:]) * root).astype(BF16)
            else:
                if b:
                    linv[o:o + 128, :o] = -dotn(
                        linv[o:o + 128, o:o + 128], dotn(a[o:o + 128, :o], linv[:o, :o])
                    )
                ln = (dott(sketch[:, :o + 128], linv[o:o + 128, :o + 128]) * root).astype(BF16)
            left[:, o:o + 128] = ln
            if first:
                lp[b] = swap_rows(ln, PHYS)
                send(lp.at[b], bout.at[b, c * 8 + x * 2 + y], zs.at[b], zr.at[b], to_left)
            lnt[...] = ln.astype(F32).T.astype(BF16)

        def last_ahead():
            o = CHI - 128
            ahead[...] = sketch[:, o:] - dott(sketch[:, :o], dotn(a[o:, :o], linv[:o, :o]))

        def partial(b, t):
            t = (t + 4 * (1 - c)) % PHYS
            cols = pl.ds(pl.multiple_of(t * CHI, CHI), CHI)
            blk = jnp.dot(lnt[...], theta[:, cols], preferred_element_type=F32)
            blk = (blk * scale).astype(BF16)
            part[b, 2 * t] = blk[:, 0:256]
            part[b, 2 * t + 1] = blk[:, 256:512]

        def to_core(b):
            core[b] = send(
                part.at[b, pl.ds((1 - c) * 8, 8)], rbc.at[b], cs.at[b], cr.at[b], c_dev
            )

        lo, hi = pl.ds(0, 64), pl.ds(64, 64)

        def hop(b, i, src, dst, dev):
            hops[b, i] = send(src, dst, ds.at[b, i], dr.at[b, i], dev)

        def step_a(b):
            core[b].wait_recv()
            half = part[b, pl.ds(c * 8, 8)].astype(F32) + rbc[b].astype(F32)
            part[b, pl.ds(c * 8, 8)] = half.astype(BF16)
            hop(b, 0, part.at[b, pl.ds(c * 8 + (1 - y) * 4, 4), lo], rby.at[b], y_dev)
            for k in range(3):
                xx = (x + k + 1) % 4
                for yy in range(2):
                    hop(b, 1 + 2 * k + yy, part.at[b, c * 8 + yy * 4 + xx, hi],
                        rbx.at[b, k, yy], x_devs[k])

        def step_b(b):
            hops[b, 0].wait_recv()
            row = pl.ds(c * 8 + y * 4, 4)
            part[b, row, lo] = (part[b, row, lo].astype(F32) + rby[b].astype(F32)).astype(BF16)
            for k in range(3):
                hop(b, 7 + k, part.at[b, c * 8 + y * 4 + (x + k + 1) % 4, lo],
                    rbx2.at[b, k], x_devs[k])
            for i in range(1, 7):
                hops[b, i].wait_recv()
            for yy in range(2):
                i = c * 8 + yy * 4 + x
                tot = (part[b, i, hi].astype(F32) + rbx[b, 0, yy].astype(F32)) + (
                    rbx[b, 1, yy].astype(F32) + rbx[b, 2, yy].astype(F32))
                part[b, i, hi] = tot.astype(BF16)
            hop(b, 10, part.at[b, c * 8 + (1 - y) * 4 + x, hi], rby2.at[b], y_dev)

        def step_d(b):
            for i in range(7, 11):
                hops[b, i].wait_recv()
            tot = (part[b, me, lo].astype(F32) + rbx2[b, 0].astype(F32)) + (
                rbx2[b, 1].astype(F32) + rbx2[b, 2].astype(F32))
            fin[b, lo] = tot.astype(BF16)
            fin[b, hi] = (part[b, me, hi].astype(F32) + rby2[b].astype(F32)).astype(BF16)
            for i in range(4):
                send(
                    fin.at[b, pl.ds(32 * i, 32)], rcol.at[me], as_.at[b, i], ar.at[me],
                    (right, 4 * b + i),
                )

        def update(b):
            o = b * 128
            if b < 2:
                rest = slice(o + 256, CHI)
                lb = dott(a[rest, o:o + 128], linv[o:o + 128, o:o + 128])
                a[rest, o:o + 128] = lb
                a[rest, o + 128:o + 256] = a[rest, o + 128:o + 256] - dott(
                    lb, a[o + 128:o + 256, o:o + 128])
                a[rest, rest] = a[rest, rest] - dott(lb, lb)

        plan = {0: {8: [lambda: sums[1].forward()]}}
        for b in range(1, 4):
            steps = {0: [functools.partial(columns, b - 1)]}
            for t in range(PHYS):
                steps.setdefault(1 + t // 2, []).append(functools.partial(partial, b - 1, t))
            steps[2].append(functools.partial(to_core, b - 1))
            steps[6] = [functools.partial(update, b - 1)]
            steps[11] = [functools.partial(step_a, b - 1)]
            if b > 1:
                steps[9] = [functools.partial(step_b, b - 2)]
            if b > 2:
                steps[7] = [functools.partial(step_d, b - 3)]
            plan[b] = steps
        plan[3].setdefault(11, []).append(last_ahead)
        for b in range(4):
            o = b * 128

            def hook(p, b=b):
                for f in plan[b].get(p, ()):
                    f()

            linv[o:o + 128, o:o + 128] = jnp.concatenate(
                leaf([a[o + 8 * q:o + 8 * q + 8, o:o + 128] for q in range(16)], hook), 0
            )
            if b == 0:
                sums[1].finish()
                unpack_rest(scr_b[3], a)
            if b < 3:
                linv[o:o + 128, o + 128:] = jnp.zeros((128, CHI - o - 128), F32)
                after = slice(o + 128, o + 256)
                lb = dott(a[after, o:o + 128], linv[o:o + 128, o:o + 128])
                a[after, o:o + 128] = lb
                a[after, after] = a[after, after] - dott(lb, lb)
        columns(3)
        for t in range(4):
            partial(3, t)
        to_core(3)
        for t in range(4, PHYS):
            partial(3, t)
        step_d(1)
        step_b(2)
        step_a(3)
        step_d(2)
        step_b(3)
        step_d(3)
        for d in sent:
            d.wait_send()

    @pl.when(jnp.logical_not(is_left))
    def _():
        if first:
            seam = (s % 8) // 7
            sent, cores = [], []

            def slot(b, k, other):
                yy = (y + other + seam) % 2
                return bout.at[b, c * 8 + ((x + 4 - k) % 4) * 2 + yy]

            def send(b, i, ref, dev):
                d = rcopy(ref, ref, gxs.at[b, i], gxr.at[b, i], dev)
                d.start()
                sent.append(d)

            def to_sibling(b, i, ref):
                d = rcopy(ref, ref, gcs.at[b, i], gcr.at[b, i], c_dev)
                d.start()
                sent.append(d)
                cores.append(d)

            def here(ref, rs):
                pltpu.make_async_copy(ref, ref, rs).wait()

            lo, hi = pl.ds(0, 128), pl.ds(128, 128)

            def one(b):
                ref = slot(b, 0, 0)
                here(ref, zr.at[b])
                send(b, 0, ref.at[lo], y_dev)
                for k in range(3):
                    send(b, 1 + k, ref.at[hi], x_devs[k])
                for k in range(3):
                    send(b, 4 + k, ref.at[lo], x_devs[k])
                send(b, 13, ref.at[hi], y_dev)
                to_sibling(b, 0, ref)

            def two(b):
                ref = slot(b, 0, 1)
                here(ref.at[lo], gxr.at[b, 0])
                for k in range(3):
                    send(b, 7 + k, ref.at[lo], x_devs[k])
                for k in range(3):
                    ref = slot(b, k + 1, 0)
                    here(ref.at[hi], gxr.at[b, 1 + k])
                    send(b, 10 + k, ref.at[hi], y_dev)

            def three(b):
                for k in range(3):
                    ref = slot(b, k + 1, 0)
                    here(ref.at[lo], gxr.at[b, 4 + k])
                    to_sibling(b, 1 + k, ref)
                ref = slot(b, 0, 1)
                here(ref.at[hi], gxr.at[b, 13])
                to_sibling(b, 4, ref)
                for k in range(3):
                    ref = slot(b, k + 1, 1)
                    here(ref.at[lo], gxr.at[b, 7 + k])
                    here(ref.at[hi], gxr.at[b, 10 + k])
                    to_sibling(b, 5 + k, ref)

            one(0)
            two(0)
            for b in range(1, 4):
                one(b)
                three(b - 1)
                two(b)
            three(3)
            for d in cores:
                d.wait_recv()
            for d in sent:
                d.wait_send()
        for q in range(16):
            pltpu.make_async_copy(rcol.at[q], rcol.at[q], ar.at[q]).wait()
        rows = jnp.concatenate(
            [jnp.concatenate([rcol[2 * t], rcol[2 * t + 1]], axis=1) for t in range(PHYS)], axis=0
        )
        left[...] = swap_rows(rows, 32)


def mid_call(pay_a, pay_b, sketch, theta, parity, cid):
    sem = pltpu.SemaphoreType.DMA
    first = parity == 0
    outs = [
        jax.ShapeDtypeStruct((256, CHI), BF16),
        jax.ShapeDtypeStruct((8, 128), F32),
    ]
    scratch = [
        pltpu.VMEM((CHI, CHI), F32), pltpu.VMEM((CHI, CHI), F32),
        pltpu.VMEM((4, 16, 128, 256), BF16), pltpu.VMEM((4, 8, 128, 256), BF16),
        pltpu.VMEM((4, 4, 64, 256), BF16), pltpu.VMEM((4, 3, 2, 64, 256), BF16),
        pltpu.VMEM((4, 64, 256), BF16), pltpu.VMEM((4, 3, 64, 256), BF16),
        pltpu.VMEM((4, 128, 256), BF16),
        pltpu.VMEM((16, 32, 256), BF16), pltpu.VMEM((128, 256), BF16),
        pltpu.VMEM((256, 128), F32),
        sem((4,)), sem((4,)), sem((4, 11)), sem((4, 11)), sem((4, 4)), sem((16,)),
    ] + sum_scratch(16) + sum_scratch(72)
    if first:
        outs.append(jax.ShapeDtypeStruct((4, 16, 256, 128), BF16))
        scratch += [
            pltpu.VMEM((4, 256, 128), BF16), sem((4,)), sem((4,)),
            sem((4, 14)), sem((4, 14)), sem((4, 8)), sem((4, 8)),
        ]
    return pl.pallas_call(
        functools.partial(mid_kernel, parity),
        name="mid%d" % cid,
        out_shape=outs,
        in_specs=[VMEM] * 4,
        out_specs=[VMEM] * len(outs),
        scratch_shapes=scratch,
        compiler_params=params(cid),
    )(pay_a, pay_b, sketch, theta)


def shards(mps, projection, gates):
    proj = projection[0]
    a = mps[0].reshape(256, CHI)
    b = gather(a, 0)
    logs = []
    for parity in range(2):
        theta, sketch, pay_a, pay_b = theta_call(a, b, proj, gates)
        a, log, *more = mid_call(pay_a, pay_b, sketch, theta, parity, parity + 1)
        b = more[0] if more else None
        logs.append(log)
    odd = lax.axis_index("site") % 2 == 1
    log = jnp.where(odd, logs[1], logs[0])
    return a.reshape(1, 32, PHYS, CHI), log[0, 0:1]


def solution(mesh):
    return jax.shard_map(
        shards,
        mesh=mesh,
        in_specs=(P("site", "bond", None, None), P("site", None, None), P()),
        out_specs=(P("site", "bond", None, None), P("site")),
        check_vma=False,
    )
```

```python
import functools
import math

import jax
import jax.numpy as jnp
from jax import lax
from jax.experimental import pallas as pl
from jax.experimental.pallas import tpu as pltpu
from jax.sharding import PartitionSpec as P

PHYS = 8
CHI = 512
epsilon = 1e-06
MESH = pl.DeviceIdType.MESH
HI = lax.Precision.HIGHEST
F32 = jnp.float32
BF16 = jnp.bfloat16
VMEM = pl.BlockSpec(memory_space=pltpu.VMEM)
ANY = pl.BlockSpec(memory_space=pl.ANY)
VLIM = 56 << 20


def params(cid=None):
    if cid is None:
        return pltpu.CompilerParams(vmem_limit_bytes=VLIM)
    return pltpu.CompilerParams(
        collective_id=cid, has_side_effects=True, vmem_limit_bytes=VLIM
    )


def place():
    s = lax.axis_index("site")
    b = lax.axis_index("bond")
    return s, b // 4, (b // 2) % 2, b % 2


def bond(x, y, c):
    return (x * 2 + y) * 2 + c


def greet(sends_to_me, count):
    barrier = pltpu.get_barrier_semaphore()
    for dev in sends_to_me:
        pl.semaphore_signal(barrier, inc=1, device_id=dev, device_id_type=MESH)
    pl.semaphore_wait(barrier, count)


def swap_rows(value, inner):
    n = value.shape[0]
    ri = lax.broadcasted_iota(jnp.int32, (n, n), 0)
    ci = lax.broadcasted_iota(jnp.int32, (n, n), 1)
    outer = n // inner
    perm = jnp.where(ci == (ri % outer) * inner + ri // outer, 1.0, 0.0).astype(BF16)
    return jnp.dot(perm, value, preferred_element_type=F32).astype(BF16)


def rcopy(src, dst, ssem, rsem, dev):
    return pltpu.make_async_remote_copy(
        src_ref=src, dst_ref=dst, send_sem=ssem, recv_sem=rsem,
        device_id=dev, device_id_type=MESH,
    )


class Ring:
    def __init__(self, out, sems, s, x, y, c, h):
        self.out, self.c = out, c
        self.ys, self.yr, self.xs, self.xr, self.cs, self.cr = sems
        self.x, self.h = x, h
        self.xp, self.xm, self.x2 = (x + 1) % 4, (x + 3) % 4, (x + 2) % 4
        self.hn = 1 - h
        self.y_dev = (s, bond(x, 1 - y, c))
        self.xp_dev = (s, bond(self.xp, y, c))
        self.xm_dev = (s, bond(self.xm, y, c))
        self.c_dev = (s, bond(x, y, 1 - c))
        self.partners = [self.y_dev, self.xp_dev, self.xm_dev, self.c_dev]
        self.started, self.core, self.ysend = [], [], []

    def slot(self, xx, yy, k):
        return self.out.at[self.c * 8 + xx * 2 + yy, pl.ds(64 * k, 64)]

    def send(self, ref, ss, rs, dev):
        d = rcopy(ref, ref, ss, rs, dev)
        d.start()
        self.started.append(d)
        return d

    def to_core(self, xx, yy, k):
        i = len(self.core)
        ref = self.slot(xx, yy, k)
        self.core.append(self.send(ref, self.cs.at[i], self.cr.at[i], self.c_dev))

    def home(self, k):
        ref = self.slot(self.x, self.h, k)
        self.ysend.append(self.send(ref, self.ys.at[k], self.yr.at[k], self.y_dev))
        for i, dev in enumerate((self.xp_dev, self.xm_dev)):
            self.send(ref, self.xs.at[i, 0, k], self.xr.at[i, 0, k], dev)
        self.to_core(self.x, self.h, k)

    def arrived(self, i, j, k, xx, yy, part):
        ref = self.slot(xx, yy, part)
        pltpu.make_async_copy(ref, ref, self.xr.at[i, j, k]).wait()

    def rest(self):
        x, h, hn, xp, xm, x2 = self.x, self.h, self.hn, self.xp, self.xm, self.x2
        xs, xr = self.xs, self.xr
        for k in range(4):
            self.ysend[k].wait_recv()
            for i, dev in enumerate((self.xp_dev, self.xm_dev)):
                self.send(self.slot(x, hn, k), xs.at[i, 1, k], xr.at[i, 1, k], dev)
            self.to_core(x, hn, k)
        for j, yy in ((0, h), (1, hn)):
            for k in range(4):
                for i, (xx, dev) in enumerate(((xm, self.xp_dev), (xp, self.xm_dev))):
                    self.arrived(i, j, k, xx, yy, k)
                    if k // 2 == i:
                        self.send(self.slot(xx, yy, k), xs.at[i, 2 + j, k], xr.at[i, 2 + j, k], dev)
                    self.to_core(xx, yy, k)
        for j, yy in ((0, h), (1, hn)):
            for k in range(4):
                self.arrived(k // 2, 2 + j, k, x2, yy, k)
                self.to_core(x2, yy, k)
        for d in self.core:
            d.wait_recv()

    def drain(self):
        for d in self.started:
            d.wait_send()


def ring_sems():
    sem = pltpu.SemaphoreType.DMA
    return [sem((4,)), sem((4,)), sem((2, 4, 4)), sem((2, 4, 4)), sem((32,)), sem((32,))]


def seams(s, x, y, c):
    h = (y + (s % 8) // 7) % 2
    to_left = ((s + 15) % 16, bond(x, (y + ((s + 7) % 8) // 7) % 2, c))
    from_right = ((s + 1) % 16, bond(x, h, c))
    return h, to_left, from_right


def gather_kernel(mine, out, own, zs, zr, *sems):
    s, x, y, c = place()
    h, to_left, from_right = seams(s, x, y, c)
    ring = Ring(out, sems, s, x, y, c, h)
    own[...] = swap_rows(mine[...], PHYS)
    greet([from_right] + ring.partners, 5)
    z = []
    for k in range(4):
        d = rcopy(
            own.at[pl.ds(64 * k, 64)], out.at[c * 8 + x * 2 + y, pl.ds(64 * k, 64)],
            zs.at[k], zr.at[k], to_left,
        )
        d.start()
        z.append(d)
    for k in range(4):
        z[k].wait_recv()
        ring.home(k)
    ring.rest()
    for d in z:
        d.wait_send()
    ring.drain()


def gather(own, cid):
    sem = pltpu.SemaphoreType.DMA
    return pl.pallas_call(
        gather_kernel,
        name="gather%d" % cid,
        out_shape=jax.ShapeDtypeStruct((16, 256, CHI), BF16),
        in_specs=[VMEM],
        out_specs=ANY,
        scratch_shapes=[pltpu.VMEM((256, CHI), BF16), sem((4,)), sem((4,))] + ring_sems(),
        compiler_params=params(cid),
    )(own)


BLOCKS = [(0, 0), (1, 0), (1, 1), (2, 0), (2, 1), (2, 2), (3, 0), (3, 1), (3, 2), (3, 3)]


def theta_kernel(a, b, proj_in, gates, theta, sketch, pay_a, pay_b, raw, proj, proj_sem):
    load = pltpu.make_async_copy(proj_in, proj, proj_sem)
    load.start()
    a_val = a[...]

    def raw_step(t, _):
        cols = pl.ds(pl.multiple_of(t * CHI, CHI), CHI)
        rows = pl.ds(pl.multiple_of(t * 32, 32), 32)
        acc = None
        for c in range(2):
            slots = [(i % 2) * 8 + i // 2 for i in range(8 * c, 8 * c + 8)]
            if len(b.shape) == 3:
                part = jnp.concatenate([b[i, rows, :] for i in slots], axis=0)
            else:
                part = jnp.concatenate(
                    [jnp.concatenate([b[k, i, rows, :] for i in slots], axis=0) for k in range(4)],
                    axis=1,
                )
            term = jnp.dot(a_val[:, c * 256:(c + 1) * 256], part, preferred_element_type=F32)
            acc = term if acc is None else acc + term
        raw[:, cols] = acc
        return 0

    lax.fori_loop(0, PHYS, raw_step, 0, unroll=4)
    gate = gates[lax.axis_index("site")]
    g_hi = gate.astype(BF16)
    g_lo = (gate - g_hi.astype(F32)).astype(BF16)
    g_hi, g_lo = [
        swap_rows(swap_rows(g, 8).astype(F32).T.astype(BF16), 8).astype(F32).T.astype(BF16)
        for g in (g_hi, g_lo)
    ]
    g3 = jnp.concatenate([g_hi, g_hi, g_lo], axis=1)

    def gate_step(i, ss):
        halves = []
        for e in range(2):
            rows = pl.ds(pl.multiple_of(i * 16, 16) + 8 * e, 8)
            xr = jnp.concatenate(
                [raw[rows, t * CHI:(t + 1) * CHI] for t in range(PHYS)], axis=0
            )
            hi = xr.astype(BF16)
            lo = (xr - hi.astype(F32)).astype(BF16)
            x3 = jnp.concatenate([hi, lo, hi], axis=0)
            g = jnp.dot(g3, x3, preferred_element_type=F32)
            for v in range(PHYS):
                gv = g[v * 8:(v + 1) * 8, :]
                ss = ss + gv * gv
            halves.append(g)
        rows = pl.ds(pl.multiple_of(i * 16, 16), 16)
        for v in range(PHYS):
            pair = jnp.concatenate([h[v * 8:(v + 1) * 8, :] for h in halves], axis=0)
            theta[rows, v * CHI:(v + 1) * CHI] = pair.astype(BF16)
        return ss

    ss = lax.fori_loop(0, 16, gate_step, jnp.zeros((8, CHI), F32), unroll=16)
    ss = (ss[:, 0:128] + ss[:, 128:256]) + (ss[:, 256:384] + ss[:, 384:512])
    load.wait()
    sk = jnp.dot(theta[...], proj[...], preferred_element_type=F32)
    sketch[...] = sk
    skt = sk.T
    for n, (bi, bj) in enumerate(BLOCKS):
        blk = lax.dot_general(
            skt[bi * 128:(bi + 1) * 128, :], sk[:, bj * 128:(bj + 1) * 128],
            (((1,), (0,)), ((), ())), precision=HI, preferred_element_type=F32,
        )
        if n == 0:
            for p in range(16):
                pay_a[p, 0:8, :] = blk[8 * p:8 * p + 8, :]
            continue
        r = 128 * (n - 1)
        while r < 128 * n:
            p, o = r // 72, r % 72
            e = min(72 - o, 128 * n - r)
            pay_b[p, o:o + e, :] = blk[r - 128 * (n - 1):r - 128 * (n - 1) + e, :]
            r += e
    for p in range(16):
        pay_a[p, 8:16, :] = ss


def theta_call(a, b, proj, gates):
    return pl.pallas_call(
        theta_kernel,
        name="theta",
        out_shape=[
            jax.ShapeDtypeStruct((256, PHYS * CHI), BF16),
            jax.ShapeDtypeStruct((256, CHI), F32),
            jax.ShapeDtypeStruct((16, 16, 128), F32),
            jax.ShapeDtypeStruct((16, 72, 128), F32),
        ],
        in_specs=[VMEM, VMEM, ANY, VMEM],
        out_specs=[VMEM] * 4,
        scratch_shapes=[
            pltpu.VMEM((256, PHYS * CHI), F32), pltpu.VMEM((PHYS * CHI, CHI), BF16),
            pltpu.SemaphoreType.DMA,
        ],
        compiler_params=params(),
    )(a, b, proj, gates)


class Sum:
    def __init__(self, pay, half, rb0, rb1, out, sems, c, me, c_dev, devs, sent):
        self.pay, self.half, self.rb0, self.rb1, self.out = pay, half, rb0, rb1, out
        self.sems, self.c, self.me, self.c_dev, self.devs = sems, c, me, c_dev, devs
        self.sent, self.cores = sent, []

    def send(self, src, dst, i, k, dev):
        d = rcopy(src, dst, self.sems[2 * i].at[k], self.sems[2 * i + 1].at[k], dev)
        d.start()
        self.sent.append(d)
        return d

    def begin(self):
        self.core = self.send(self.pay.at[pl.ds((1 - self.c) * 8, 8)], self.rb0, 0, 0, self.c_dev)

    def scatter(self):
        self.core.wait_recv()
        self.half[...] = self.pay[pl.ds(self.c * 8, 8)] + self.rb0[...]
        self.parts = [
            self.send(self.half.at[(self.me + k + 1) % 8], self.rb1.at[k], 1, k, dev)
            for k, dev in enumerate(self.devs)
        ]

    def spread(self):
        for d in self.parts:
            d.wait_recv()
        t = [self.rb1[k] for k in range(7)]
        slot = self.c * 8 + self.me
        self.out[slot] = ((self.half[self.me] + t[0]) + (t[1] + t[2])) + (
            (t[3] + t[4]) + (t[5] + t[6]))
        ref = self.out.at[slot]
        self.wide = [self.send(ref, ref, 2, k, dev) for k, dev in enumerate(self.devs)]
        self.cores.append(self.send(ref, ref, 3, 7, self.c_dev))

    def forward(self):
        for k in range(7):
            self.wide[k].wait_recv()
            ref = self.out.at[self.c * 8 + (self.me + 7 - k) % 8]
            self.cores.append(self.send(ref, ref, 3, k, self.c_dev))

    def finish(self):
        for d in self.cores:
            d.wait_recv()


def sum_scratch(rows):
    sem = pltpu.SemaphoreType.DMA
    return [
        pltpu.VMEM((8, rows, 128), F32), pltpu.VMEM((8, rows, 128), F32),
        pltpu.VMEM((7, rows, 128), F32), pltpu.VMEM((16, rows, 128), F32),
        sem((1,)), sem((1,)), sem((7,)), sem((7,)), sem((7,)), sem((7,)), sem((8,)), sem((8,)),
    ]


def bl(v, k):
    return jnp.broadcast_to(v[:, k:k + 1], (8, 128))


def bs(v, j):
    return jnp.broadcast_to(v[j:j + 1, :], (8, 128))


def leaf(rows, hook):
    lane = lax.broadcasted_iota(jnp.int32, (8, 128), 1)
    sub = lax.broadcasted_iota(jnp.int32, (8, 128), 0)
    rows = list(rows)
    out = []
    n = len(rows)
    for p in range(n):
        m_p = rows[p]
        c = [bl(m_p, 8 * p + v) for v in range(8)]
        pc = (lane >= 8 * p) & (lane < 8 * p + 8)
        m_p = jnp.where(pc, jnp.where(lane - 8 * p == sub, 1.0, 0.0), m_p)
        fwd = m_p
        diag = None
        for j in range(8):
            d = bs(c[j], j)
            isj = sub == j
            mult = jnp.where(isj, 0.0, c[j] * (1.0 / d))
            if j:
                diag = jnp.where(isj, d, diag)
                fwd = jnp.where(isj, m_p, fwd)
            else:
                diag = d
            for v in range(j + 1, 8):
                c[v] = c[v] - mult * bs(c[v], j)
            m_p = m_p - mult * bs(m_p, j)
        out.append(jnp.where(lane < 8 * p + 8, fwd * lax.rsqrt(diag), 0.0))
        if p == n - 1:
            break
        yy = m_p * (1.0 / diag)
        yb = [bs(yy, v) for v in range(8)]
        for q in range(p + 1, n):
            t = [bl(rows[q], 8 * p + v) * yb[v] for v in range(8)]
            tot = ((t[0] + t[1]) + (t[2] + t[3])) + ((t[4] + t[5]) + (t[6] + t[7]))
            rows[q] = jnp.where(pc, 0.0, rows[q]) - tot
        hook(p)
    return out


def dott(a, b):
    return lax.dot_general(
        a, b, (((1,), (1,)), ((), ())), precision=HI, preferred_element_type=F32
    )


def dotn(a, b):
    return lax.dot_general(
        a, b, (((1,), (0,)), ((), ())), precision=HI, preferred_element_type=F32
    )


def unpack_rest(pay, a):
    for n, (bi, bj) in enumerate(BLOCKS[1:]):
        r = 128 * n
        while r < 128 * n + 128:
            p, o = r // 72, r % 72
            e = min(72 - o, 128 * n + 128 - r)
            q = bi * 128 + r - 128 * n
            a[q:q + e, bj * 128:(bj + 1) * 128] = pay[p, o:o + e, :]
            r += e


def mid_kernel(parity, *refs):
    first = parity == 0
    refs = list(refs)
    pay_a, pay_b, sketch, theta, left, log = refs[:6]
    refs = refs[6:]
    if first:
        bout, lp, zs, zr, gxs, gxr, gcs, gcr = refs[:1] + refs[-7:]
        refs = refs[1:-7]
    a, linv, part, rbc, rby, rbx, rby2, rbx2, fin, rcol, lnt, ahead = refs[:12]
    cs, cr, ds, dr, as_, ar = refs[12:18]
    scr_a, scr_b = refs[18:30], refs[30:42]

    s, x, y, c = place()
    is_left = s % 2 == parity
    _, to_left, from_right = seams(s, x, y, c)
    c_dev = (s, bond(x, y, 1 - c))
    right, before = (s + 1) % 16, (s + 15) % 16
    others = [(x * 2 + y + k) % 8 for k in range(1, 8)]
    greet(
        [c_dev] + [(s, bond(q // 2, q % 2, c)) for q in others]
        + [(before, q) for q in range(16)] + ([from_right] if first else []),
        25 if first else 24,
    )
    me = c * 8 + y * 4 + x
    y_dev = (s, bond(x, 1 - y, c))
    x_devs = [(s, bond((x + k) % 4, y, c)) for k in range(1, 4)]
    root = math.sqrt(PHYS * CHI)

    @pl.when(is_left)
    def _():
        sent = []

        def send(src, dst, ss, rs, dev):
            d = rcopy(src, dst, ss, rs, dev)
            d.start()
            sent.append(d)
            return d

        devs = [(s, bond(q // 2, q % 2, c)) for q in others]
        sums = [
            Sum(pay, *scr[:4], scr[4:], c, x * 2 + y, c_dev, devs, sent)
            for pay, scr in ((pay_a, scr_a), (pay_b, scr_b))
        ]
        for f in ("begin", "scatter", "spread"):
            for v in sums:
                getattr(v, f)()
        sums[0].forward()
        sums[0].finish()
        gram = scr_a[3]
        total = jnp.sum(jnp.sum(gram[0, 8:16, :], axis=0, keepdims=True), axis=1, keepdims=True)
        mean_square = total * (1.0 / (CHI * PHYS * PHYS * CHI)) + epsilon
        log[...] = jnp.broadcast_to(0.5 * jnp.log(mean_square), (8, 128))
        scale = lax.rsqrt(mean_square) * (1.0 / root)
        for p in range(16):
            a[8 * p:8 * p + 8, 0:128] = gram[p, 0:8, :]
        core, hops = {}, {}

        def columns(b):
            o = b * 128
            if b == 3:
                ln = (dott(ahead[...], linv[o:, o:]) * root).astype(BF16)
            else:
                if b:
                    linv[o:o + 128, :o] = -dotn(
                        linv[o:o + 128, o:o + 128], dotn(a[o:o + 128, :o], linv[:o, :o])
                    )
                ln = (dott(sketch[:, :o + 128], linv[o:o + 128, :o + 128]) * root).astype(BF16)
            left[:, o:o + 128] = ln
            if first:
                lp[b] = swap_rows(ln, PHYS)
                send(lp.at[b], bout.at[b, c * 8 + x * 2 + y], zs.at[b], zr.at[b], to_left)
            lnt[...] = ln.astype(F32).T.astype(BF16)

        def last_ahead():
            o = CHI - 128
            ahead[...] = sketch[:, o:] - dott(sketch[:, :o], dotn(a[o:, :o], linv[:o, :o]))

        def partial(b, t):
            t = (t + 4 * (1 - c)) % PHYS
            cols = pl.ds(pl.multiple_of(t * CHI, CHI), CHI)
            blk = jnp.dot(lnt[...], theta[:, cols], preferred_element_type=F32)
            blk = (blk * scale).astype(BF16)
            part[b, 2 * t] = blk[:, 0:256]
            part[b, 2 * t + 1] = blk[:, 256:512]

        def to_core(b):
            core[b] = send(
                part.at[b, pl.ds((1 - c) * 8, 8)], rbc.at[b], cs.at[b], cr.at[b], c_dev
            )

        lo, hi = pl.ds(0, 64), pl.ds(64, 64)

        def hop(b, i, src, dst, dev):
            hops[b, i] = send(src, dst, ds.at[b, i], dr.at[b, i], dev)

        def step_a(b):
            core[b].wait_recv()
            half = part[b, pl.ds(c * 8, 8)].astype(F32) + rbc[b].astype(F32)
            part[b, pl.ds(c * 8, 8)] = half.astype(BF16)
            hop(b, 0, part.at[b, pl.ds(c * 8 + (1 - y) * 4, 4), lo], rby.at[b], y_dev)
            for k in range(3):
                xx = (x + k + 1) % 4
                for yy in range(2):
                    hop(b, 1 + 2 * k + yy, part.at[b, c * 8 + yy * 4 + xx, hi],
                        rbx.at[b, k, yy], x_devs[k])

        def step_b(b):
            hops[b, 0].wait_recv()
            row = pl.ds(c * 8 + y * 4, 4)
            part[b, row, lo] = (part[b, row, lo].astype(F32) + rby[b].astype(F32)).astype(BF16)
            for k in range(3):
                hop(b, 7 + k, part.at[b, c * 8 + y * 4 + (x + k + 1) % 4, lo],
                    rbx2.at[b, k], x_devs[k])
            for i in range(1, 7):
                hops[b, i].wait_recv()
            for yy in range(2):
                i = c * 8 + yy * 4 + x
                tot = (part[b, i, hi].astype(F32) + rbx[b, 0, yy].astype(F32)) + (
                    rbx[b, 1, yy].astype(F32) + rbx[b, 2, yy].astype(F32))
                part[b, i, hi] = tot.astype(BF16)
            hop(b, 10, part.at[b, c * 8 + (1 - y) * 4 + x, hi], rby2.at[b], y_dev)

        def step_d(b):
            for i in range(7, 11):
                hops[b, i].wait_recv()
            tot = (part[b, me, lo].astype(F32) + rbx2[b, 0].astype(F32)) + (
                rbx2[b, 1].astype(F32) + rbx2[b, 2].astype(F32))
            fin[b, lo] = tot.astype(BF16)
            fin[b, hi] = (part[b, me, hi].astype(F32) + rby2[b].astype(F32)).astype(BF16)
            for i in range(4):
                send(
                    fin.at[b, pl.ds(32 * i, 32)], rcol.at[me], as_.at[b, i], ar.at[me],
                    (right, 4 * b + i),
                )

        def update(b):
            o = b * 128
            if b < 2:
                rest = slice(o + 256, CHI)
                lb = dott(a[rest, o:o + 128], linv[o:o + 128, o:o + 128])
                a[rest, o:o + 128] = lb
                a[rest, o + 128:o + 256] = a[rest, o + 128:o + 256] - dott(
                    lb, a[o + 128:o + 256, o:o + 128])
                a[rest, rest] = a[rest, rest] - dott(lb, lb)

        plan = {0: {8: [lambda: sums[1].forward()]}}
        for b in range(1, 4):
            steps = {0: [functools.partial(columns, b - 1)]}
            for t in range(PHYS):
                steps.setdefault(1 + t // 2, []).append(functools.partial(partial, b - 1, t))
            steps[2].append(functools.partial(to_core, b - 1))
            steps[6] = [functools.partial(update, b - 1)]
            steps[11] = [functools.partial(step_a, b - 1)]
            if b > 1:
                steps[9] = [functools.partial(step_b, b - 2)]
            if b > 2:
                steps[7] = [functools.partial(step_d, b - 3)]
            plan[b] = steps
        plan[3].setdefault(11, []).append(last_ahead)
        for b in range(4):
            o = b * 128

            def hook(p, b=b):
                for f in plan[b].get(p, ()):
                    f()

            linv[o:o + 128, o:o + 128] = jnp.concatenate(
                leaf([a[o + 8 * q:o + 8 * q + 8, o:o + 128] for q in range(16)], hook), 0
            )
            if b == 0:
                sums[1].finish()
                unpack_rest(scr_b[3], a)
            if b < 3:
                linv[o:o + 128, o + 128:] = jnp.zeros((128, CHI - o - 128), F32)
                after = slice(o + 128, o + 256)
                lb = dott(a[after, o:o + 128], linv[o:o + 128, o:o + 128])
                a[after, o:o + 128] = lb
                a[after, after] = a[after, after] - dott(lb, lb)
        columns(3)
        for t in range(4):
            partial(3, t)
        to_core(3)
        for t in range(4, PHYS):
            partial(3, t)
        step_d(1)
        step_b(2)
        step_a(3)
        step_d(2)
        step_b(3)
        step_d(3)
        for d in sent:
            d.wait_send()

    @pl.when(jnp.logical_not(is_left))
    def _():
        if first:
            seam = (s % 8) // 7
            sent, cores = [], []

            def slot(b, k, other):
                yy = (y + other + seam) % 2
                return bout.at[b, c * 8 + ((x + 4 - k) % 4) * 2 + yy]

            def send(b, i, ref, dev):
                d = rcopy(ref, ref, gxs.at[b, i], gxr.at[b, i], dev)
                d.start()
                sent.append(d)

            def to_sibling(b, i, ref):
                d = rcopy(ref, ref, gcs.at[b, i], gcr.at[b, i], c_dev)
                d.start()
                sent.append(d)
                cores.append(d)

            def here(ref, rs):
                pltpu.make_async_copy(ref, ref, rs).wait()

            lo, hi = pl.ds(0, 128), pl.ds(128, 128)

            def one(b):
                ref = slot(b, 0, 0)
                here(ref, zr.at[b])
                send(b, 0, ref.at[lo], y_dev)
                for k in range(3):
                    send(b, 1 + k, ref.at[hi], x_devs[k])
                for k in range(3):
                    send(b, 4 + k, ref.at[lo], x_devs[k])
                send(b, 13, ref.at[hi], y_dev)
                to_sibling(b, 0, ref)

            def two(b):
                ref = slot(b, 0, 1)
                here(ref.at[lo], gxr.at[b, 0])
                for k in range(3):
                    send(b, 7 + k, ref.at[lo], x_devs[k])
                for k in range(3):
                    ref = slot(b, k + 1, 0)
                    here(ref.at[hi], gxr.at[b, 1 + k])
                    send(b, 10 + k, ref.at[hi], y_dev)

            def three(b):
                for k in range(3):
                    ref = slot(b, k + 1, 0)
                    here(ref.at[lo], gxr.at[b, 4 + k])
                    to_sibling(b, 1 + k, ref)
                ref = slot(b, 0, 1)
                here(ref.at[hi], gxr.at[b, 13])
                to_sibling(b, 4, ref)
                for k in range(3):
                    ref = slot(b, k + 1, 1)
                    here(ref.at[lo], gxr.at[b, 7 + k])
                    here(ref.at[hi], gxr.at[b, 10 + k])
                    to_sibling(b, 5 + k, ref)

            one(0)
            two(0)
            for b in range(1, 4):
                one(b)
                three(b - 1)
                two(b)
            three(3)
            for d in cores:
                d.wait_recv()
            for d in sent:
                d.wait_send()
        for q in range(16):
            pltpu.make_async_copy(rcol.at[q], rcol.at[q], ar.at[q]).wait()
        rows = jnp.concatenate(
            [jnp.concatenate([rcol[2 * t], rcol[2 * t + 1]], axis=1) for t in range(PHYS)], axis=0
        )
        left[...] = swap_rows(rows, 32)


def mid_call(pay_a, pay_b, sketch, theta, parity, cid):
    sem = pltpu.SemaphoreType.DMA
    first = parity == 0
    outs = [
        jax.ShapeDtypeStruct((256, CHI), BF16),
        jax.ShapeDtypeStruct((8, 128), F32),
    ]
    scratch = [
        pltpu.VMEM((CHI, CHI), F32), pltpu.VMEM((CHI, CHI), F32),
        pltpu.VMEM((4, 16, 128, 256), BF16), pltpu.VMEM((4, 8, 128, 256), BF16),
        pltpu.VMEM((4, 4, 64, 256), BF16), pltpu.VMEM((4, 3, 2, 64, 256), BF16),
        pltpu.VMEM((4, 64, 256), BF16), pltpu.VMEM((4, 3, 64, 256), BF16),
        pltpu.VMEM((4, 128, 256), BF16),
        pltpu.VMEM((16, 32, 256), BF16), pltpu.VMEM((128, 256), BF16),
        pltpu.VMEM((256, 128), F32),
        sem((4,)), sem((4,)), sem((4, 11)), sem((4, 11)), sem((4, 4)), sem((16,)),
    ] + sum_scratch(16) + sum_scratch(72)
    if first:
        outs.append(jax.ShapeDtypeStruct((4, 16, 256, 128), BF16))
        scratch += [
            pltpu.VMEM((4, 256, 128), BF16), sem((4,)), sem((4,)),
            sem((4, 14)), sem((4, 14)), sem((4, 8)), sem((4, 8)),
        ]
    return pl.pallas_call(
        functools.partial(mid_kernel, parity),
        name="mid%d" % cid,
        out_shape=outs,
        in_specs=[VMEM] * 4,
        out_specs=[VMEM] * len(outs),
        scratch_shapes=scratch,
        compiler_params=params(cid),
    )(pay_a, pay_b, sketch, theta)


def shards(mps, projection, gates):
    proj = projection[0]
    a = mps[0].reshape(256, CHI)
    b = gather(a, 0)
    logs = []
    for parity in range(2):
        theta, sketch, pay_a, pay_b = theta_call(a, b, proj, gates)
        a, log, *more = mid_call(pay_a, pay_b, sketch, theta, parity, parity + 1)
        b = more[0] if more else None
        logs.append(log)
    odd = lax.axis_index("site") % 2 == 1
    log = jnp.where(odd, logs[1], logs[0])
    return a.reshape(1, 32, PHYS, CHI), log[0, 0:1]


def solution(mesh):
    return jax.shard_map(
        shards,
        mesh=mesh,
        in_specs=(P("site", "bond", None, None), P("site", None, None), P()),
        out_specs=(P("site", "bond", None, None), P("site")),
        check_vma=False,
    )
```
